32 devices in a mesh: row: 4 (over z), col: 4 (over y, x), pair: 2 (over core).
Axes of the slice: x: 2, y: 2, z: 4, core: 2. Of those that a mesh axis runs over, the one named last changes fastest.
Arguments:
- integrals: bfloat16 [2048, 2048], P('row', ('col', 'pair')), may hold values from -0.1875 to 0.1875
- int_mask: int32 [32, 32], P('row', ('col', 'pair')), may hold values 0 or 1
- amplitudes: bfloat16 [2048, 2048], P('row', ('col', 'pair')), may hold values from -6 to 6
- domain_mask: int32 [32, 2048], P('row', ('col', 'pair')), may hold values 0 or 1
- virt_energy: float32 [2048], P('row'), may hold values from 0.5 to 4
- occ_energy: float32 [2048], P(('col', 'pair')), may hold values from -3 to -0.5
Outputs:
- update: float32 [2048, 2048], P('row', ('col', 'pair'))
The draws below stay inside these ranges and needn't reach their ends.
All inputs are finite; a program needn't handle non-finite values. No bound on the sum of `int_mask` or of `domain_mask` on one device may be relied on, other than what follows from the above.
Results may differ from the reference program's by a relative error of at most 0.0003.
Values may be sent and summed in bfloat16 or wider, within the bound.
A program may use at most 64 MiB of HBM per device.

```python
import math
import jax
import jax.numpy as jnp

TILE = 64
NC = 2048
NP = 2048


def with_ends(entries, key, least, high):
    shape = entries.shape
    place = [jax.random.randint(jax.random.fold_in(key, axis), (), 0, shape[axis]) for axis in range(len(shape))]
    entries = entries.at[tuple(place)].set(least)
    longest = shape.index(max(shape))
    place[longest] = (place[longest] + 1) % shape[longest]
    return entries.at[tuple(place)].set(high)


def shard_levels(rng, dims, pieces, low, high):
    loudness, own = 1.0, jax.random.fold_in(rng, 6)
    for dim, shards_of in pieces:
        draws = jnp.exp(jax.random.uniform(jax.random.fold_in(own, dim), (shards_of,), jnp.float32, low / len(pieces), high / len(pieces)))
        loudness = loudness * jnp.repeat(draws, dims[dim] // shards_of).reshape([-1 if axis == dim else 1 for axis in range(len(dims))])
    return loudness


def centred(key, extent, width, reach, shards=(), kind=jnp.bfloat16):
    values = width * jax.random.normal(key, extent, jnp.float32)
    if shards:
        values = values * shard_levels(key, extent, shards, -0.22, 0.18)
    return jnp.clip(values, -reach, reach).astype(kind)


def setup_inputs(seed: int = 0) -> dict:
    keys = jax.random.split(jax.random.key(seed), 7)
    integrals = centred(keys[0], (NC, NC), (NC // 2) ** -0.5, 0.1875, ((0, 4), (1, 8)))
    int_mask = with_ends((jax.random.randint(keys[1], (NC // TILE, NC // TILE), 0, 2) < 1).astype(jnp.int32), jax.random.fold_in(keys[1], 1), 0, 1)
    amplitudes = centred(keys[2], (NC, NP), 1.0, 6.0, ((0, 4), (1, 8)))
    domain_mask = with_ends((jax.random.randint(keys[3], (NC // TILE, NP), 0, 4) < 3).astype(jnp.int32), jax.random.fold_in(keys[3], 1), 0, 1)
    virt_energy = jnp.clip(jnp.exp(math.log(4.0) - 2.0794415 * jax.random.uniform(keys[4], (NC,), jnp.float32) ** shard_levels(keys[4], (NC,), ((0, 4),), -0.2, 0.2)), 0.5, 4.0)
    occ_energy = jnp.clip(-3.0 + 2.5 * jax.random.uniform(keys[5], (NP,), jnp.float32) ** shard_levels(keys[5], (NP,), ((0, 8),), -0.2, 0.2), -3.0, -0.5)
    return dict(integrals=integrals, int_mask=int_mask, amplitudes=amplitudes, domain_mask=domain_mask, virt_energy=virt_energy, occ_energy=occ_energy)


def reference(integrals, int_mask, amplitudes, domain_mask, virt_energy, occ_energy):
    count_rows = integrals.shape[0] // TILE
    count_cols = integrals.shape[1] // TILE
    masked_ints = (integrals.reshape(count_rows, TILE, count_cols, TILE)
                   * int_mask[:, None, :, None].astype(integrals.dtype)).reshape(integrals.shape)
    pairs = amplitudes.shape[1]
    row_mask = domain_mask[:, None, :].astype(amplitudes.dtype)
    masked_amps = (amplitudes.reshape(count_rows, TILE, pairs) * row_mask).reshape(amplitudes.shape)
    ladder = jnp.dot(masked_ints, masked_amps, preferred_element_type=jnp.float32)
    denominator = virt_energy[:, None] - occ_energy[None, :]
    scaled = ladder / denominator
    out_mask = domain_mask[:, None, :].astype(jnp.float32)
    return (scaled.reshape(count_rows, TILE, pairs) * out_mask).reshape(scaled.shape)
```

```python
import functools

import jax
import jax.numpy as jnp
from jax import lax
from jax.experimental import pallas as pl
from jax.experimental.pallas import tpu as pltpu
from jax.sharding import PartitionSpec as P

TILE = 64
PIECES = 1
MESH = pl.DeviceIdType.MESH


def flipped(index, distance, count):
    out, bit = 0, 1
    while bit < count:
        have = lax.rem(index // bit, 2)
        out = out + bit * (1 - have if (distance // bit) % 2 else have)
        bit *= 2
    return out


def kernel(R, C, a_hbm, im_hbm, b_hbm, dm_hbm, v_hbm, o_hbm, out_ref,
           a_all, b_all, acc, inv, im_ref, dm_ref, v_ref, o_ref, load_sem, store_sem,
           a_send, a_recv, sib_send, sib_recv, dn_send, dn_recv, up_send, up_recv):
    r, c, p = lax.axis_index("row"), lax.axis_index("col"), lax.axis_index("pair")
    q = 1 - p
    me = c * 2 + p
    rows, width = a_hbm.shape
    depth, cols = b_hbm.shape
    parts = depth // width
    half = rows // 2
    bits = [1 << i for i in range(C.bit_length() - 1)]

    loads = [
        pltpu.make_async_copy(src, dst, load_sem.at[i]) for i, (src, dst) in enumerate([
            (dm_hbm, dm_ref), (b_hbm, b_all.at[r]), (im_hbm, im_ref), (a_hbm, a_all.at[me]),
            (v_hbm, v_ref), (o_hbm, o_ref)])
    ]
    for load in loads:
        load.start()

    others = [flipped(c, d, C) for d in range(C)]
    barrier = pltpu.get_barrier_semaphore()

    def greet(device):
        pl.semaphore_signal(barrier, inc=1, device_id=device, device_id_type=MESH)

    greet((r, c, q))
    for e in bits:
        greet((r, others[e], p))

    @pl.when(r > 0)
    def _():
        greet((r - 1, c, p))

    @pl.when(r < R - 1)
    def _():
        greet((r + 1, c, p))

    def part(block, j):
        return b_all.at[block, pl.ds(j * width, width)]

    def down(block, s, j):
        return pltpu.make_async_remote_copy(
            src_ref=part(block, j), dst_ref=part(block, j),
            send_sem=dn_send.at[s, j], recv_sem=dn_recv.at[s, j],
            device_id=(r - 1, c, p), device_id_type=MESH)

    def up(block, s, j):
        return pltpu.make_async_remote_copy(
            src_ref=part(block, j), dst_ref=part(block, j),
            send_sem=up_send.at[s, j], recv_sem=up_recv.at[s, j],
            device_id=(r + 1, c, p), device_id_type=MESH)

    def across(d, e, h):
        piece = a_all.at[others[d] * 2 + p, pl.ds(h * half, half)]
        return pltpu.make_async_remote_copy(
            src_ref=piece, dst_ref=piece,
            send_sem=a_send.at[d + e, h], recv_sem=a_recv.at[d + e, h],
            device_id=(r, others[e], p), device_id_type=MESH)

    def sibling(d, h, core=None):
        piece = a_all.at[others[d] * 2 + (p if core is None else core), pl.ds(h * half, half)]
        return pltpu.make_async_remote_copy(
            src_ref=piece, dst_ref=piece,
            send_sem=sib_send.at[d, h], recv_sem=sib_recv.at[d, h],
            device_id=(r, c, q), device_id_type=MESH)

    def onward(d, h):
        if d == 0:
            return bits
        low, high = d & -d, 1 << (d.bit_length() - 1)
        return [e for e in bits if (e < low if h == 0 else e > high)]

    def arrives(d, h):
        low, high = d & -d, 1 << (d.bit_length() - 1)
        e = low if h == 0 else high
        piece = a_all.at[others[d] * 2 + p, pl.ds(h * half, half)]
        pltpu.make_async_remote_copy(
            src_ref=piece, dst_ref=piece,
            send_sem=a_send.at[d, h], recv_sem=a_recv.at[d, h],
            device_id=(r, others[e], p), device_id_type=MESH).wait_recv()
        for e in onward(d, h):
            across(d, e, h).start()
        sibling(d, h).start()

    loads[0].wait()
    loads[1].wait()
    for t in range(depth // TILE):
        keep = dm_ref[t:t + 1, :].astype(jnp.bfloat16)
        here = pl.ds(t * TILE, TILE)
        b_all[r, here, :] = b_all[r, here, :] * keep

    pl.semaphore_wait(barrier, 1 + len(bits) + (r + R - 1) // R + (2 * R - 2 - r) // R)

    for j in range(parts):
        @pl.when(r > 0)
        def _():
            down(r, 0, j).start()

        @pl.when(r < R - 1)
        def _():
            up(r, 0, j).start()

    loads[2].wait()
    loads[3].wait()
    lane = lax.broadcasted_iota(jnp.int32, (1, width), 1) // TILE
    for t in range(rows // TILE):
        keep = jnp.zeros((1, width), jnp.float32)
        for u in range(width // TILE):
            keep = jnp.where(lane == u, im_ref[u:u + 1, t:t + 1].astype(jnp.float32), keep)
        here = pl.ds(t * TILE, TILE)
        a_all[me, here, :] = a_all[me, here, :] * keep.astype(jnp.bfloat16)

    for h in (1, 0):
        for e in bits:
            g = h if 2 * e < C else 1 - h
            across(0, e, g).start()
    for h in range(2):
        sibling(0, h).start()

    loads[4].wait()
    loads[5].wait()
    for t in range(rows // 128):
        v = jnp.broadcast_to(v_ref[:, t * 128:(t + 1) * 128], (128, 128)).T
        for u in range(cols // 128):
            lanes = slice(u * 128, (u + 1) * 128)
            factor = 1.0 / (v - o_ref[:, lanes])
            for w in range(128 // TILE):
                row = t * (128 // TILE) + w
                keep = dm_ref[row:row + 1, lanes].astype(jnp.float32)
                inv[pl.ds(row * TILE, TILE), lanes] = factor[w * TILE:(w + 1) * TILE] * keep

    def receive(s, j):
        above, below = r + s + 1, r - s - 1

        @pl.when(above < R)
        def _():
            down(above, s, j).wait_recv()

            @pl.when(r > 0)
            def _():
                down(above, s + 1, j).start()

        @pl.when(below >= 0)
        def _():
            up(below, s, j).wait_recv()

            @pl.when(r < R - 1)
            def _():
                up(below, s + 1, j).start()

    whole = pl.ds(0, rows)

    def product(block, j, here=whole):
        return jnp.dot(a_all[block * parts + j, here, :], b_all[block, j * width:(j + 1) * width],
                       preferred_element_type=jnp.float32)

    def add(s, j, here=whole):
        @pl.when(r + s + 1 < R)
        def _():
            acc[here, :] += product(r + s + 1, j, here)

        @pl.when(r - s - 1 >= 0)
        def _():
            acc[here, :] += product(r - s - 1, j, here)

    along = [(0, j) for j in range(parts)]
    near = [d for d in range(1, C) if d in bits]
    for h in (1, 0):
        for d in near:
            arrives(d, h if 2 * d < C else 1 - h)
        if along:
            receive(*along.pop(0))
    while along:
        receive(*along.pop(0))
    for d in sorted(range(1, C), key=lambda d: d.bit_count()):
        if d not in near:
            for h in range(2):
                arrives(d, h)
    later = [(s, j) for s in range(1, R - 1) for j in range(parts)]
    if later:
        receive(*later[0])
    for d in range(C):
        for h in range(2):
            sibling(d, h, q).wait_recv()

    acc[...] = product(r, 0)
    for j in range(1, parts):
        acc[...] += product(r, j)
    due = [(0, j) for j in range(parts)]
    for item in later[:1]:
        add(*due.pop(0))
        due.append(item)
    for item in later[1:]:
        if item == later[-1]:
            while due:
                add(*due.pop(0))
        receive(*item)
        due.append(item)
        if item != later[-1]:
            add(*due.pop(0))

    stores = []
    for t in range(PIECES):
        here = pl.ds(t * (rows // PIECES), rows // PIECES)
        for s, j in due:
            add(s, j, here)
        acc[here, :] = acc[here, :] * inv[here, :]
        out_ref[here, :] = acc[here, :]

    for d in range(C):
        for h in range(2):
            sibling(d, h).wait_send()
            for e in onward(d, h):
                across(d, e, h).wait_send()
    for s in range(R - 1):
        for j in range(parts):
            @pl.when((r + s < R) & (r > 0))
            def _():
                down(r + s, s, j).wait_send()

            @pl.when((r - s >= 0) & (r < R - 1))
            def _():
                up(r - s, s, j).wait_send()
    for store in stores:
        store.wait()


def solution(mesh):
    R, C = mesh.shape["row"], mesh.shape["col"]

    def local(integrals, int_mask, amplitudes, domain_mask, virt_energy, occ_energy):
        rows, width = integrals.shape
        depth, cols = amplitudes.shape
        parts = depth // width
        hbm = pl.BlockSpec(memory_space=pl.ANY)
        dma = pltpu.SemaphoreType.DMA
        return pl.pallas_call(
            functools.partial(kernel, R, C),
            out_shape=pltpu.VMEM((rows, cols), jnp.float32),
            in_specs=[hbm] * 6,
            out_specs=pl.BlockSpec(memory_space=pltpu.VMEM),
            scratch_shapes=[
                pltpu.VMEM((C * 2, rows, width), jnp.bfloat16),
                pltpu.VMEM((R, depth, cols), jnp.bfloat16),
                pltpu.VMEM((rows, cols), jnp.float32),
                pltpu.VMEM((rows, cols), jnp.float32),
                pltpu.VMEM(int_mask.shape[::-1], jnp.int32),
                pltpu.VMEM(domain_mask.shape, jnp.int32),
                pltpu.VMEM((1, rows), jnp.float32),
                pltpu.VMEM((1, cols), jnp.float32),
                dma((6,)), dma((PIECES,)), dma((C, 2)), dma((C, 2)), dma((C, 2)), dma((C, 2)),
                dma((R - 1, parts)), dma((R - 1, parts)), dma((R - 1, parts)), dma((R - 1, parts)),
            ],
            compiler_params=pltpu.CompilerParams(
                collective_id=0, has_side_effects=True, vmem_limit_bytes=32 * 2**20),
            cost_estimate=pl.CostEstimate(
                flops=2 * rows * depth * R * cols, bytes_accessed=4 * 2**20, transcendentals=0),
        )(*[pltpu.with_memory_space_constraint(z, pltpu.HBM) for z in (integrals, int_mask.T, amplitudes, domain_mask,
          virt_energy.reshape(1, rows), occ_energy.reshape(1, cols))])

    placed = (
        P("row", ("col", "pair")),
        P("row", ("col", "pair")),
        P("row", ("col", "pair")),
        P("row", ("col", "pair")),
        P("row"),
        P(("col", "pair")),
    )
    return jax.shard_map(
        local, mesh=mesh, in_specs=placed, out_specs=P("row", ("col", "pair")), check_vma=False
    )
```

```python
import functools

import jax
import jax.numpy as jnp
from jax import lax
from jax.experimental import pallas as pl
from jax.experimental.pallas import tpu as pltpu
from jax.sharding import PartitionSpec as P

TILE = 64
SPLIT = 2
MESH = pl.DeviceIdType.MESH


def flipped(index, distance, count):
    out, bit = 0, 1
    while bit < count:
        have = lax.rem(index // bit, 2)
        out = out + bit * (1 - have if (distance // bit) % 2 else have)
        bit *= 2
    return out


def kernel(R, C, a_hbm, im_hbm, b_hbm, dm_hbm, v_hbm, o_hbm, acc,
           a_all, b_all, inv, im_ref, dm_ref, dm_above, v_ref, o_ref, load_sem,
           a_send, a_recv, sib_send, sib_recv, dn_send, dn_recv, up_send, up_recv, dm_send, dm_recv,
           above_in, plane_in, go):
    r, c, p = lax.axis_index("row"), lax.axis_index("col"), lax.axis_index("pair")
    q = 1 - p
    me = c * 2 + p
    rows, width = a_hbm.shape
    depth, cols = b_hbm.shape
    parts = depth // width
    pieces = parts * SPLIT
    tall = depth // pieces
    half = rows // 2
    bits = [1 << i for i in range(C.bit_length() - 1)]
    others = [flipped(c, d, C) for d in range(C)]

    loads = [
        pltpu.make_async_copy(src, dst, load_sem.at[i]) for i, (src, dst) in enumerate([
            (dm_hbm, dm_ref), (b_hbm, b_all.at[r]), (im_hbm, im_ref), (a_hbm, a_all.at[me]),
            (v_hbm, v_ref), (o_hbm, o_ref)])
    ]

    barrier = pltpu.get_barrier_semaphore()

    def greet(device):
        pl.semaphore_signal(barrier, inc=1, device_id=device, device_id_type=MESH)

    @pl.when(r < R - 1)
    def _():
        greet((r + 1, c, p))

    @pl.when(p == 1)
    def _():
        for e in bits:
            greet((r, others[e], p))

        @pl.when(r > 0)
        def _():
            greet((r - 1, c, p))

    @pl.when(p == 0)
    def _():
        greet((r, c, q))

    for load in loads:
        load.start()

    @pl.when(p == 1)
    def _():
        pl.semaphore_wait(barrier, (r + R - 1) // R + (2 * R - 2 - r) // R + len(bits) + 1)

    @pl.when((p == 0) & (r > 0))
    def _():
        pl.semaphore_wait(barrier, 1)
        pl.semaphore_signal(above_in, inc=1, device_id=(r - 1, c, p), device_id_type=MESH)

    @pl.when(p == 1)
    def _():
        for e in bits:
            pl.semaphore_signal(plane_in, inc=1, device_id=(r, others[e], p), device_id_type=MESH)

    def strip(block, j):
        return b_all.at[block, pl.ds(j * tall, tall)]

    def down(block, s, j):
        return pltpu.make_async_remote_copy(
            src_ref=strip(block, j), dst_ref=strip(block, j),
            send_sem=dn_send.at[s, j], recv_sem=dn_recv.at[s, j],
            device_id=(r - 1, c, p), device_id_type=MESH)

    def up(block, s, j):
        return pltpu.make_async_remote_copy(
            src_ref=strip(block, j), dst_ref=strip(block, j),
            send_sem=up_send.at[s, j], recv_sem=up_recv.at[s, j],
            device_id=(r + 1, c, p), device_id_type=MESH)

    def raw(j):
        return pltpu.make_async_remote_copy(
            src_ref=b_hbm.at[pl.ds(j * tall, tall)], dst_ref=strip(r, j),
            send_sem=dn_send.at[0, j], recv_sem=dn_recv.at[0, j],
            device_id=(r - 1, c, p), device_id_type=MESH)

    def domains():
        return pltpu.make_async_remote_copy(
            src_ref=dm_hbm, dst_ref=dm_above, send_sem=dm_send, recv_sem=dm_recv,
            device_id=(r - 1, c, p), device_id_type=MESH)

    def across(d, e, h):
        piece = a_all.at[others[d] * 2 + p, pl.ds(h * half, half)]
        return pltpu.make_async_remote_copy(
            src_ref=piece, dst_ref=piece,
            send_sem=a_send.at[d + e, h], recv_sem=a_recv.at[d + e, h],
            device_id=(r, others[e], p), device_id_type=MESH)

    def sibling(d, h, core=None):
        piece = a_all.at[others[d] * 2 + (p if core is None else core), pl.ds(h * half, half)]
        return pltpu.make_async_remote_copy(
            src_ref=piece, dst_ref=piece,
            send_sem=sib_send.at[d, h], recv_sem=sib_recv.at[d, h],
            device_id=(r, c, q), device_id_type=MESH)

    def onward(d, h):
        if d == 0:
            return bits
        low, high = d & -d, 1 << (d.bit_length() - 1)
        return [e for e in bits if (e < low if h == 0 else e > high)]

    def arrives(d, h):
        low, high = d & -d, 1 << (d.bit_length() - 1)
        e = low if h == 0 else high
        piece = a_all.at[others[d] * 2 + p, pl.ds(h * half, half)]
        pltpu.make_async_remote_copy(
            src_ref=piece, dst_ref=piece,
            send_sem=a_send.at[d, h], recv_sem=a_recv.at[d, h],
            device_id=(r, others[e], p), device_id_type=MESH).wait_recv()
        for e in onward(d, h):
            across(d, e, h).start()
        sibling(d, h).start()

    def mask(block, j, domain):
        for t in range(j * tall // TILE, (j + 1) * tall // TILE):
            here = pl.ds(t * TILE, TILE)
            b_all[block, here, :] = b_all[block, here, :] * domain[t:t + 1, :].astype(jnp.bfloat16)

    @pl.when(r == 1)
    def _():
        raw(0).start()
        domains().start()
        for j in range(1, pieces):
            raw(j).start()

    loads[0].wait()
    loads[1].wait()
    for j in range(pieces):
        mask(r, j, dm_ref)

        @pl.when(r > 1)
        def _():
            down(r, 0, j).start()

    @pl.when((p == 0) & (r < R - 1))
    def _():
        pl.semaphore_wait(above_in, 1)

    @pl.when(r < R - 1)
    def _():
        for j in range(pieces):
            up(r, 0, j).start()

    @pl.when(p == 1)
    def _():
        pl.semaphore_wait(plane_in, len(bits))
        pl.semaphore_signal(go, inc=1, device_id=(r, c, q), device_id_type=MESH)

    loads[2].wait()
    loads[3].wait()
    lane = lax.broadcasted_iota(jnp.int32, (1, width), 1) // TILE
    for t in range(rows // TILE):
        keep = jnp.zeros((1, width), jnp.float32)
        for u in range(width // TILE):
            keep = jnp.where(lane == u, im_ref[u:u + 1, t:t + 1].astype(jnp.float32), keep)
        here = pl.ds(t * TILE, TILE)
        a_all[me, here, :] = a_all[me, here, :] * keep.astype(jnp.bfloat16)

    @pl.when(p == 0)
    def _():
        pl.semaphore_wait(go, 1)

    for h in (1, 0):
        for e in bits:
            g = h if 2 * e < C else 1 - h
            across(0, e, g).start()
    for h in range(2):
        sibling(0, h).start()

    loads[4].wait()
    loads[5].wait()
    for t in range(rows // 128):
        v = jnp.broadcast_to(v_ref[:, t * 128:(t + 1) * 128], (128, 128)).T
        for u in range(cols // 128):
            lanes = slice(u * 128, (u + 1) * 128)
            factor = 1.0 / (v - o_ref[:, lanes])
            for w in range(128 // TILE):
                row = t * (128 // TILE) + w
                keep = dm_ref[row:row + 1, lanes].astype(jnp.float32)
                inv[pl.ds(row * TILE, TILE), lanes] = factor[w * TILE:(w + 1) * TILE] * keep

    def receive(s, j):
        above, below = r + s + 1, r - s - 1

        @pl.when(above < R)
        def _():
            down(above, s, j).wait_recv()

            @pl.when(r > 0)
            def _():
                down(above, s + 1, j).start()

            if s == 0:
                @pl.when(r == 0)
                def _():
                    if j == 0:
                        domains().wait_recv()
                    mask(1, j, dm_above)

        @pl.when(below >= 0)
        def _():
            up(below, s, j).wait_recv()

            @pl.when(r < R - 1)
            def _():
                up(below, s + 1, j).start()

    def product(block, j, part=0, of=1):
        deep = width // of
        k = pl.ds(j * width + part * deep, deep)
        return jnp.dot(a_all[block * parts + j, :, part * deep:(part + 1) * deep], b_all[block, k, :],
                       preferred_element_type=jnp.float32)

    def add(s, j):
        @pl.when(r + s + 1 < R)
        def _():
            acc[...] += product(r + s + 1, j)

        @pl.when(r - s - 1 >= 0)
        def _():
            acc[...] += product(r - s - 1, j)

    strips = [(s, j) for s in range(R - 1) for j in range(pieces)]

    def take(count):
        for _ in range(count):
            if len(strips) > SPLIT:
                receive(*strips.pop(0))

    near = [d for d in range(1, C) if d in bits]
    take(2)
    for h in (1, 0):
        for d in near:
            arrives(d, h if 2 * d < C else 1 - h)
        take(2)
    for d in sorted(range(1, C), key=lambda d: d.bit_count()):
        if d not in near:
            for h in range(2):
                arrives(d, h)
    take(1)
    for d in range(C):
        for h in range(2):
            sibling(d, h, q).wait_recv()

    acc[...] = product(r, 0)
    for j in range(1, parts):
        acc[...] += product(r, j)
    whole = [(s, j) for s in range(R - 1) for j in range(parts)]
    for s, j in whole[:-1]:
        while strips and strips[0] <= (s, (j + 1) * SPLIT - 1):
            receive(*strips.pop(0))
        add(s, j)

    s, j = whole[-1]
    for i in range(SPLIT - 1):
        receive(s, j * SPLIT + i)

        @pl.when(r == 0)
        def _():
            acc[...] += product(R - 1, j, i, SPLIT)

        @pl.when(r == R - 1)
        def _():
            acc[...] += product(0, j, i, SPLIT)

    receive(s, pieces - 1)

    @pl.when(r == 0)
    def _():
        acc[...] = (acc[...] + product(R - 1, j, SPLIT - 1, SPLIT)) * inv[...]

    @pl.when(r == R - 1)
    def _():
        acc[...] = (acc[...] + product(0, j, SPLIT - 1, SPLIT)) * inv[...]

    @pl.when((r > 0) & (r < R - 1))
    def _():
        acc[...] = acc[...] * inv[...]

    for d in range(C):
        for h in range(2):
            sibling(d, h).wait_send()
            for e in onward(d, h):
                across(d, e, h).wait_send()
    for s in range(R - 1):
        for j in range(pieces):
            @pl.when((r + s < R) & (r > 0))
            def _():
                down(r + s, s, j).wait_send()

            @pl.when((r - s >= 0) & (r < R - 1))
            def _():
                up(r - s, s, j).wait_send()

    @pl.when(r == 1)
    def _():
        domains().wait_send()


def solution(mesh):
    R, C = mesh.shape["row"], mesh.shape["col"]

    def local(integrals, int_mask, amplitudes, domain_mask, virt_energy, occ_energy):
        rows, width = integrals.shape
        depth, cols = amplitudes.shape
        pieces = depth // width * SPLIT
        hbm = pl.BlockSpec(memory_space=pl.ANY)
        dma = pltpu.SemaphoreType.DMA
        operands = (integrals, int_mask.T, amplitudes, domain_mask,
                    virt_energy.reshape(1, rows), occ_energy.reshape(1, cols))
        return pl.pallas_call(
            functools.partial(kernel, R, C),
            out_shape=pltpu.VMEM((rows, cols), jnp.float32),
            in_specs=[hbm] * 6,
            out_specs=pl.BlockSpec(memory_space=pltpu.VMEM),
            scratch_shapes=[
                pltpu.VMEM((C * 2, rows, width), jnp.bfloat16),
                pltpu.VMEM((R, depth, cols), jnp.bfloat16),
                pltpu.VMEM((rows, cols), jnp.float32),
                pltpu.VMEM(int_mask.shape[::-1], jnp.int32),
                pltpu.VMEM(domain_mask.shape, jnp.int32),
                pltpu.VMEM(domain_mask.shape, jnp.int32),
                pltpu.VMEM((1, rows), jnp.float32),
                pltpu.VMEM((1, cols), jnp.float32),
                dma((6,)), dma((C, 2)), dma((C, 2)), dma((C, 2)), dma((C, 2)),
                dma((R - 1, pieces)), dma((R - 1, pieces)), dma((R - 1, pieces)), dma((R - 1, pieces)),
                dma, dma,
                pltpu.SemaphoreType.REGULAR, pltpu.SemaphoreType.REGULAR, pltpu.SemaphoreType.REGULAR,
            ],
            compiler_params=pltpu.CompilerParams(
                collective_id=0, has_side_effects=True, vmem_limit_bytes=32 * 2**20),
            cost_estimate=pl.CostEstimate(
                flops=2 * rows * depth * R * cols, bytes_accessed=4 * 2**20, transcendentals=0),
        )(*[pltpu.with_memory_space_constraint(x, pltpu.HBM) for x in operands])

    placed = (
        P("row", ("col", "pair")),
        P("row", ("col", "pair")),
        P("row", ("col", "pair")),
        P("row", ("col", "pair")),
        P("row"),
        P(("col", "pair")),
    )
    return jax.shard_map(
        local, mesh=mesh, in_specs=placed, out_specs=P("row", ("col", "pair")), check_vma=False
    )
```

```python
import functools

import jax
import jax.numpy as jnp
from jax import lax
from jax.experimental import pallas as pl
from jax.experimental.pallas import tpu as pltpu
from jax.sharding import PartitionSpec as P

TILE = 64
SPLIT = 2
FIRST = 1
LENT = 64
HELPER = 3
MESH = pl.DeviceIdType.MESH


def flipped(index, distance, count):
    out, bit = 0, 1
    while bit < count:
        have = lax.rem(index // bit, 2)
        out = out + bit * (1 - have if (distance // bit) % 2 else have)
        bit *= 2
    return out


def kernel(R, C, a_hbm, im_hbm, b_hbm, dm_hbm, v_hbm, o_hbm, acc,
           a_all, b_all, inv, im_ref, dm_ref, dm_above, v_ref, o_ref, load_sem,
           a_send, a_recv, sib_send, sib_recv, dn_send, dn_recv, up_send, up_recv, dm_send, dm_recv,
           lent, lend_send, lend_recv, pass_send, pass_recv, above_in, plane_in, go):
    r, c, p = lax.axis_index("row"), lax.axis_index("col"), lax.axis_index("pair")
    q = 1 - p
    me = c * 2 + p
    rows, width = a_hbm.shape
    depth, cols = b_hbm.shape
    parts = depth // width
    pieces = parts * SPLIT
    tall = depth // pieces
    half = rows // 2
    bits = [1 << i for i in range(C.bit_length() - 1)]
    others = [flipped(c, d, C) for d in range(C)]
    first = depth - LENT
    giver, taker = (r == 1) & (c == 0), (r == 0) & (c == 0)
    helper = (r == 1) & (c == HELPER) & (p == 1)

    loads = [
        pltpu.make_async_copy(src, dst, load_sem.at[i]) for i, (src, dst) in enumerate([
            (dm_hbm, dm_ref), (b_hbm, b_all.at[r]), (im_hbm, im_ref), (a_hbm, a_all.at[me]),
            (v_hbm, v_ref), (o_hbm, o_ref)])
    ]

    barrier = pltpu.get_barrier_semaphore()

    def greet(device):
        pl.semaphore_signal(barrier, inc=1, device_id=device, device_id_type=MESH)

    @pl.when(r < R - 1)
    def _():
        greet((r + 1, c, p))

    @pl.when(p == 1)
    def _():
        for e in bits:
            greet((r, others[e], p))

    @pl.when(p == 0)
    def _():
        greet((r, c, q))

    for load in loads:
        load.start()

    @pl.when(p == 1)
    def _():
        pl.semaphore_wait(barrier, (r + R - 1) // R + len(bits) + 1)

    @pl.when((p == 0) & (r > 0))
    def _():
        pl.semaphore_wait(barrier, 1)

    def strip(block, j):
        return b_all.at[block, pl.ds(j * tall, tall)]

    def down(block, s, j):
        return pltpu.make_async_remote_copy(
            src_ref=strip(block, j), dst_ref=strip(block, j),
            send_sem=dn_send.at[s, j], recv_sem=dn_recv.at[s, j],
            device_id=(r - 1, c, p), device_id_type=MESH)

    def up(block, s, j):
        return pltpu.make_async_remote_copy(
            src_ref=strip(block, j), dst_ref=strip(block, j),
            send_sem=up_send.at[s, j], recv_sem=up_recv.at[s, j],
            device_id=(r + 1, c, p), device_id_type=MESH)

    def raw(j):
        return pltpu.make_async_remote_copy(
            src_ref=b_hbm.at[pl.ds(j * tall, tall)], dst_ref=strip(r, j),
            send_sem=dn_send.at[0, j], recv_sem=dn_recv.at[0, j],
            device_id=(r - 1, c, p), device_id_type=MESH)

    def cut():
        here = pl.ds((pieces - 1) * tall, tall - LENT)
        return pltpu.make_async_remote_copy(
            src_ref=b_hbm.at[here], dst_ref=b_all.at[1, here],
            send_sem=dn_send.at[0, pieces - 1], recv_sem=dn_recv.at[0, pieces - 1],
            device_id=(0, c, p), device_id_type=MESH)

    def lend(core):
        return pltpu.make_async_remote_copy(
            src_ref=b_hbm.at[pl.ds(first, LENT)], dst_ref=lent.at[core],
            send_sem=lend_send, recv_sem=lend_recv.at[core],
            device_id=(1, HELPER, 1), device_id_type=MESH)

    def pass_on(core):
        return pltpu.make_async_remote_copy(
            src_ref=lent.at[core], dst_ref=b_all.at[1, pl.ds(first, LENT)],
            send_sem=pass_send.at[core], recv_sem=pass_recv,
            device_id=(0, 0, core), device_id_type=MESH)

    def domains():
        return pltpu.make_async_remote_copy(
            src_ref=dm_hbm, dst_ref=dm_above, send_sem=dm_send, recv_sem=dm_recv,
            device_id=(r - 1, c, p), device_id_type=MESH)

    def across(d, e, h):
        piece = a_all.at[others[d] * 2 + p, pl.ds(h * half, half)]
        return pltpu.make_async_remote_copy(
            src_ref=piece, dst_ref=piece,
            send_sem=a_send.at[d + e, h], recv_sem=a_recv.at[d + e, h],
            device_id=(r, others[e], p), device_id_type=MESH)

    def sibling(d, h, core=None):
        piece = a_all.at[others[d] * 2 + (p if core is None else core), pl.ds(h * half, half)]
        return pltpu.make_async_remote_copy(
            src_ref=piece, dst_ref=piece,
            send_sem=sib_send.at[d, h], recv_sem=sib_recv.at[d, h],
            device_id=(r, c, q), device_id_type=MESH)

    def onward(d, h):
        if d == 0:
            return bits
        low, high = d & -d, 1 << (d.bit_length() - 1)
        return [e for e in bits if (e < low if h == 0 else e > high)]

    def arrives(d, h):
        low, high = d & -d, 1 << (d.bit_length() - 1)
        e = low if h == 0 else high
        piece = a_all.at[others[d] * 2 + p, pl.ds(h * half, half)]
        pltpu.make_async_remote_copy(
            src_ref=piece, dst_ref=piece,
            send_sem=a_send.at[d, h], recv_sem=a_recv.at[d, h],
            device_id=(r, others[e], p), device_id_type=MESH).wait_recv()
        for e in onward(d, h):
            across(d, e, h).start()
        sibling(d, h).start()

    def mask(block, start, end, domain):
        for t in range(start // TILE, end // TILE):
            here = pl.ds(t * TILE, TILE)
            b_all[block, here, :] = b_all[block, here, :] * domain[t:t + 1, :].astype(jnp.bfloat16)

    @pl.when(r == 1)
    def _():
        raw(0).start()
        domains().start()
        for j in range(1, pieces - 1):
            raw(j).start()

    @pl.when(giver)
    def _():
        cut().start()

    @pl.when((r == 1) & (c > 0))
    def _():
        raw(pieces - 1).start()

    @pl.when(r > 0)
    def _():
        pl.semaphore_signal(above_in, inc=1, device_id=(r - 1, c, p), device_id_type=MESH)

    @pl.when(p == 1)
    def _():
        for e in bits:
            pl.semaphore_signal(plane_in, inc=1, device_id=(r, others[e], p), device_id_type=MESH)

    loads[0].wait()
    loads[1].wait()
    for j in range(pieces):
        mask(r, j * tall, (j + 1) * tall, dm_ref)

        @pl.when(r > 1)
        def _():
            down(r, 0, j).start()

    @pl.when(p == 1)
    def _():
        pl.semaphore_wait(plane_in, len(bits))
        pl.semaphore_signal(go, inc=1, device_id=(r, c, q), device_id_type=MESH)

    def rise():
        @pl.when(r < R - 1)
        def _():
            pl.semaphore_wait(above_in, 1)
            for j in range(pieces):
                up(r, 0, j).start()

    @pl.when(p == 0)
    def _():
        rise()

    loads[2].wait()
    loads[3].wait()
    lane = lax.broadcasted_iota(jnp.int32, (1, width), 1) // TILE
    for t in range(rows // TILE):
        keep = jnp.zeros((1, width), jnp.float32)
        for u in range(width // TILE):
            keep = jnp.where(lane == u, im_ref[u:u + 1, t:t + 1].astype(jnp.float32), keep)
        here = pl.ds(t * TILE, TILE)
        a_all[me, here, :] = a_all[me, here, :] * keep.astype(jnp.bfloat16)

    @pl.when(p == 0)
    def _():
        pl.semaphore_wait(go, 1)

    @pl.when(giver)
    def _():
        lend(p).start()

    for h in (1, 0):
        for e in bits:
            g = h if 2 * e < C else 1 - h
            across(0, e, g).start()
    for h in range(2):
        sibling(0, h).start()

    @pl.when(p == 1)
    def _():
        rise()

    loads[4].wait()
    loads[5].wait()
    for t in range(rows // 128):
        v = jnp.broadcast_to(v_ref[:, t * 128:(t + 1) * 128], (128, 128)).T
        for u in range(cols // 128):
            lanes = slice(u * 128, (u + 1) * 128)
            factor = 1.0 / (v - o_ref[:, lanes])
            for w in range(128 // TILE):
                row = t * (128 // TILE) + w
                keep = dm_ref[row:row + 1, lanes].astype(jnp.float32)
                inv[pl.ds(row * TILE, TILE), lanes] = factor[w * TILE:(w + 1) * TILE] * keep

    def receive(s, j):
        above, below = r + s + 1, r - s - 1

        short = (s, j) == (0, pieces - 1)
        if short:
            @pl.when(taker)
            def _():
                cut().wait_recv()

        @pl.when((above < R) & jnp.logical_not(taker) if short else above < R)
        def _():
            down(above, s, j).wait_recv()

            @pl.when(r > 0)
            def _():
                down(above, s + 1, j).start()

        if s == 0:
            @pl.when(r == 0)
            def _():
                if j == 0:
                    domains().wait_recv()
                mask(1, j * tall, min((j + 1) * tall, first), dm_above)

        @pl.when(below >= 0)
        def _():
            up(below, s, j).wait_recv()

            @pl.when(r < R - 1)
            def _():
                up(below, s + 1, j).start()

    def product(block, j, part=0, of=1):
        deep = width // of
        k = pl.ds(j * width + part * deep, deep)
        return jnp.dot(a_all[block * parts + j, :, part * deep:(part + 1) * deep], b_all[block, k, :],
                       preferred_element_type=jnp.float32)

    def add(s, j):
        @pl.when(r + s + 1 < R)
        def _():
            acc[...] += product(r + s + 1, j)

        @pl.when(r - s - 1 >= 0)
        def _():
            acc[...] += product(r - s - 1, j)

    strips = [(s, j) for s in range(R - 1) for j in range(pieces)]

    def take(count):
        for _ in range(min(count, len(strips) - pieces)):
            receive(*strips.pop(0))

    near = [d for d in range(1, C) if d in bits]
    take(FIRST * SPLIT)
    for h in (1, 0):
        for d in near:
            arrives(d, h if 2 * d < C else 1 - h)
        if h:
            @pl.when(helper)
            def _():
                for core in range(2):
                    lend(core).wait_recv()
                    pass_on(core).start()
        take(SPLIT)
    for d in sorted(range(1, C), key=lambda d: d.bit_count()):
        if d not in near:
            for h in range(2):
                arrives(d, h)
    take(len(strips))

    @pl.when(taker)
    def _():
        pass_on(p).wait_recv()

    @pl.when(r == 0)
    def _():
        mask(1, first, depth, dm_above)

    for d in range(C):
        for h in range(2):
            sibling(d, h, q).wait_recv()

    acc[...] = product(r, 0)
    for j in range(1, parts):
        acc[...] += product(r, j)
    whole = [(s, j) for s in range(R - 1) for j in range(parts)]
    for s, j in whole[:-1]:
        while strips and strips[0] <= (s, (j + 1) * SPLIT - 1):
            receive(*strips.pop(0))
        add(s, j)

    for d in range(C):
        for h in range(2):
            sibling(d, h).wait_send()
            for e in onward(d, h):
                across(d, e, h).wait_send()

    @pl.when((r == 0) & (R > 1))
    def _():
        for j in range(pieces):
            up(r, 0, j).wait_send()

    @pl.when((r == R - 1) & (R > 1))
    def _():
        for j in range(pieces):
            down(r, 0, j).wait_send()

    def sent():
        for s in range(R - 1):
            for j in range(pieces):
                short = (s, j) == (0, pieces - 1)

                @pl.when((r + s < R) & (r > 0) & (jnp.logical_not(giver) if short else True))
                def _():
                    down(r + s, s, j).wait_send()

                @pl.when((r - s >= 0) & (r < R - 1))
                def _():
                    up(r - s, s, j).wait_send()

        @pl.when(r == 1)
        def _():
            domains().wait_send()

        @pl.when(giver)
        def _():
            cut().wait_send()
            lend(p).wait_send()

        @pl.when(helper)
        def _():
            for core in range(2):
                pass_on(core).wait_send()

    s, j = whole[-1]
    for i in range(SPLIT - 1):
        receive(s, j * SPLIT + i)

        @pl.when(r == 0)
        def _():
            acc[...] += product(R - 1, j, i, SPLIT)

        @pl.when(r == R - 1)
        def _():
            acc[...] += product(0, j, i, SPLIT)

    receive(s, pieces - 1)

    @pl.when(r == 0)
    def _():
        acc[...] = (acc[...] + product(R - 1, j, SPLIT - 1, SPLIT)) * inv[...]

    @pl.when(r == R - 1)
    def _():
        acc[...] = (acc[...] + product(0, j, SPLIT - 1, SPLIT)) * inv[...]

    @pl.when((r > 0) & (r < R - 1))
    def _():
        acc[...] = acc[...] * inv[...]

    @pl.when((r > 0) & (r < R - 1))
    def _():
        sent()


def solution(mesh):
    R, C = mesh.shape["row"], mesh.shape["col"]

    def local(integrals, int_mask, amplitudes, domain_mask, virt_energy, occ_energy):
        rows, width = integrals.shape
        depth, cols = amplitudes.shape
        pieces = depth // width * SPLIT
        hbm = pl.BlockSpec(memory_space=pl.ANY)
        dma = pltpu.SemaphoreType.DMA
        operands = (integrals, int_mask.T, amplitudes, domain_mask,
                    virt_energy.reshape(1, rows), occ_energy.reshape(1, cols))
        return pl.pallas_call(
            functools.partial(kernel, R, C),
            out_shape=pltpu.VMEM((rows, cols), jnp.float32),
            in_specs=[hbm] * 6,
            out_specs=pl.BlockSpec(memory_space=pltpu.VMEM),
            scratch_shapes=[
                pltpu.VMEM((C * 2, rows, width), jnp.bfloat16),
                pltpu.VMEM((R, depth, cols), jnp.bfloat16),
                pltpu.VMEM((rows, cols), jnp.float32),
                pltpu.VMEM(int_mask.shape[::-1], jnp.int32),
                pltpu.VMEM(domain_mask.shape, jnp.int32),
                pltpu.VMEM(domain_mask.shape, jnp.int32),
                pltpu.VMEM((1, rows), jnp.float32),
                pltpu.VMEM((1, cols), jnp.float32),
                dma((6,)), dma((C, 2)), dma((C, 2)), dma((C, 2)), dma((C, 2)),
                dma((R - 1, pieces)), dma((R - 1, pieces)), dma((R - 1, pieces)), dma((R - 1, pieces)),
                dma, dma, pltpu.VMEM((2, LENT, cols), jnp.bfloat16), dma, dma((2,)), dma((2,)), dma,
                pltpu.SemaphoreType.REGULAR, pltpu.SemaphoreType.REGULAR, pltpu.SemaphoreType.REGULAR,
            ],
            compiler_params=pltpu.CompilerParams(
                collective_id=0, has_side_effects=True, vmem_limit_bytes=32 * 2**20),
            cost_estimate=pl.CostEstimate(
                flops=2 * rows * depth * R * cols, bytes_accessed=4 * 2**20, transcendentals=0),
        )(*[pltpu.with_memory_space_constraint(x, pltpu.HBM) for x in operands])

    placed = (
        P("row", ("col", "pair")),
        P("row", ("col", "pair")),
        P("row", ("col", "pair")),
        P("row", ("col", "pair")),
        P("row"),
        P(("col", "pair")),
    )
    return jax.shard_map(
        local, mesh=mesh, in_specs=placed, out_specs=P("row", ("col", "pair")), check_vma=False
    )
```

```python
import functools

import jax
import jax.numpy as jnp
from jax import lax
from jax.experimental import pallas as pl
from jax.experimental.pallas import tpu as pltpu
from jax.sharding import PartitionSpec as P

TILE = 64
SPLIT = 2
FIRST = 1
LENT = 64
HELPER = 3
MESH = pl.DeviceIdType.MESH


def flipped(index, distance, count):
    out, bit = 0, 1
    while bit < count:
        have = lax.rem(index // bit, 2)
        out = out + bit * (1 - have if (distance // bit) % 2 else have)
        bit *= 2
    return out


def arrivals(R, pieces):
    place, count = {}, 0
    for s in range(R - 1):
        own = list(range(pieces)) if s < R - 2 else [0] * (pieces - 1) + [1]
        for upward in (0, 1):
            if upward and 2 * s + 2 > R - 1:
                count -= own[-1] + 1
            for j in range(pieces):
                place[upward, s, j] = count + own[j]
            count += own[-1] + 1
    return place, count


def kernel(R, C, a_hbm, im_hbm, b_hbm, dm_hbm, v_hbm, o_hbm, acc,
           a_all, b_all, inv, im_ref, dm_ref, dm_above, v_ref, o_ref,
           lent, load_sem, a_sent, a_recv, sib_recv, b_sent, b_recv, dm_recv, above_in, plane_in):
    r, c, p = lax.axis_index("row"), lax.axis_index("col"), lax.axis_index("pair")
    q = 1 - p
    me = c * 2 + p
    rows, width = a_hbm.shape
    depth, cols = b_hbm.shape
    parts = depth // width
    pieces = parts * SPLIT
    tall = depth // pieces
    half = rows // 2
    place, _ = arrivals(R, pieces)
    bits = [1 << i for i in range(C.bit_length() - 1)]
    others = [flipped(c, d, C) for d in range(C)]
    first = depth - LENT
    giver = (r == 1) & (c == 0)
    helper = (r == 1) & (c == HELPER) & (p == 1)

    loads = [
        pltpu.make_async_copy(src, dst, load_sem.at[i]) for i, (src, dst) in enumerate([
            (dm_hbm, dm_ref), (b_hbm, b_all.at[r]), (im_hbm, im_ref), (a_hbm, a_all.at[me]),
            (v_hbm, v_ref), (o_hbm, o_ref)])
    ]

    barrier = pltpu.get_barrier_semaphore()

    def greet(device):
        pl.semaphore_signal(barrier, inc=1, device_id=device, device_id_type=MESH)

    @pl.when(r < R - 1)
    def _():
        greet((r + 1, c, p))

    @pl.when(p == 1)
    def _():
        for e in bits:
            greet((r, others[e], p))

    @pl.when(p == 0)
    def _():
        greet((r, c, q))

    for load in loads:
        load.start()

    @pl.when(p == 1)
    def _():
        pl.semaphore_wait(barrier, (r + R - 1) // R + len(bits) + 1)

    @pl.when((p == 0) & (r > 0))
    def _():
        pl.semaphore_wait(barrier, 1)

    def strip(block, j):
        return b_all.at[block, pl.ds(j * tall, tall)]

    def down(block, s, j):
        return pltpu.make_async_remote_copy(
            src_ref=strip(block, j), dst_ref=strip(block, j),
            send_sem=b_sent, recv_sem=b_recv.at[place[0, s, j]],
            device_id=(r - 1, c, p), device_id_type=MESH)

    def up(block, s, j):
        return pltpu.make_async_remote_copy(
            src_ref=strip(block, j), dst_ref=strip(block, j),
            send_sem=b_sent, recv_sem=b_recv.at[place[1, s, j]],
            device_id=(r + 1, c, p), device_id_type=MESH)

    def raw(j):
        return pltpu.make_async_remote_copy(
            src_ref=b_hbm.at[pl.ds(j * tall, tall)], dst_ref=strip(r, j),
            send_sem=b_sent, recv_sem=b_recv.at[place[0, 0, j]],
            device_id=(r - 1, c, p), device_id_type=MESH)

    def cut():
        here = pl.ds((pieces - 1) * tall, tall - LENT)
        return pltpu.make_async_remote_copy(
            src_ref=b_hbm.at[here], dst_ref=b_all.at[1, here],
            send_sem=b_sent, recv_sem=b_recv.at[place[0, 0, pieces - 1]],
            device_id=(0, c, p), device_id_type=MESH)

    def lend(core):
        return pltpu.make_async_remote_copy(
            src_ref=b_hbm.at[pl.ds(first, LENT)], dst_ref=lent.at[core],
            send_sem=b_sent, recv_sem=a_recv.at[0, core],
            device_id=(1, HELPER, 1), device_id_type=MESH)

    def pass_on(core):
        return pltpu.make_async_remote_copy(
            src_ref=lent.at[core], dst_ref=b_all.at[1, pl.ds(first, LENT)],
            send_sem=load_sem.at[1], recv_sem=b_recv.at[place[0, 0, pieces - 1]],
            device_id=(0, 0, core), device_id_type=MESH)

    def domains():
        return pltpu.make_async_remote_copy(
            src_ref=dm_ref, dst_ref=dm_above, send_sem=load_sem.at[0], recv_sem=dm_recv,
            device_id=(r - 1, c, p), device_id_type=MESH)

    def across(d, e, h):
        piece = a_all.at[others[d] * 2 + p, pl.ds(h * half, half)]
        return pltpu.make_async_remote_copy(
            src_ref=piece, dst_ref=piece,
            send_sem=a_sent, recv_sem=a_recv.at[d + e, h],
            device_id=(r, others[e], p), device_id_type=MESH)

    def sibling(d, h):
        piece = a_all.at[others[d] * 2 + p, pl.ds(h * half, half)]
        return pltpu.make_async_remote_copy(
            src_ref=piece, dst_ref=piece,
            send_sem=a_sent, recv_sem=sib_recv,
            device_id=(r, c, q), device_id_type=MESH)

    def await_blocks(count, sem):
        blocks = a_all.at[pl.ds(0, count)]
        pltpu.make_async_copy(blocks, blocks, sem).wait()

    def onward(d, h):
        if d == 0:
            return bits
        low, high = d & -d, 1 << (d.bit_length() - 1)
        return [e for e in bits if (e < low if h == 0 else e > high)]

    def arrives(d, h):
        low, high = d & -d, 1 << (d.bit_length() - 1)
        e = low if h == 0 else high
        piece = a_all.at[others[d] * 2 + p, pl.ds(h * half, half)]
        pltpu.make_async_remote_copy(
            src_ref=piece, dst_ref=piece,
            send_sem=a_sent, recv_sem=a_recv.at[d, h],
            device_id=(r, others[e], p), device_id_type=MESH).wait_recv()
        for e in onward(d, h):
            across(d, e, h).start()
        sibling(d, h).start()

    def mask(block, start, end, domain):
        for t in range(start // TILE, end // TILE):
            here = pl.ds(t * TILE, TILE)
            b_all[block, here, :] = b_all[block, here, :] * domain[t:t + 1, :].astype(jnp.bfloat16)

    @pl.when(r == 1)
    def _():
        for j in range(pieces - 1):
            raw(j).start()

    @pl.when(giver)
    def _():
        cut().start()

    @pl.when((r == 1) & (c > 0))
    def _():
        raw(pieces - 1).start()

    @pl.when(r > 0)
    def _():
        pl.semaphore_signal(above_in, inc=1, device_id=(r - 1, c, p), device_id_type=MESH)

    @pl.when(p == 1)
    def _():
        for e in bits:
            pl.semaphore_signal(plane_in, inc=1, device_id=(r, others[e], p), device_id_type=MESH)

    loads[0].wait()
    loads[1].wait()

    @pl.when(r == 1)
    def _():
        domains().start()

    for j in range(pieces):
        mask(r, j * tall, (j + 1) * tall, dm_ref)

        @pl.when(r > 1)
        def _():
            down(r, 0, j).start()

    @pl.when(p == 1)
    def _():
        pl.semaphore_wait(plane_in, len(bits))
        pl.semaphore_signal(plane_in, inc=1, device_id=(r, c, q), device_id_type=MESH)

    def rise():
        @pl.when(r < R - 1)
        def _():
            pl.semaphore_wait(above_in, 1)
            for j in range(pieces):
                up(r, 0, j).start()

    @pl.when(p == 0)
    def _():
        rise()

    loads[2].wait()
    loads[3].wait()
    lane = lax.broadcasted_iota(jnp.int32, (1, width), 1) // TILE
    for t in range(rows // TILE):
        keep = jnp.zeros((1, width), jnp.float32)
        for u in range(width // TILE):
            keep = jnp.where(lane == u, im_ref[u:u + 1, t:t + 1].astype(jnp.float32), keep)
        here = pl.ds(t * TILE, TILE)
        a_all[me, here, :] = a_all[me, here, :] * keep.astype(jnp.bfloat16)

    @pl.when(p == 0)
    def _():
        pl.semaphore_wait(plane_in, 1)

    @pl.when(giver)
    def _():
        lend(p).start()

    for h in (1, 0):
        for e in bits:
            g = h if 2 * e < C else 1 - h
            across(0, e, g).start()
    for h in range(2):
        sibling(0, h).start()

    @pl.when(p == 1)
    def _():
        rise()

    loads[4].wait()
    loads[5].wait()
    for t in range(rows // 128):
        v = jnp.broadcast_to(v_ref[:, t * 128:(t + 1) * 128], (128, 128)).T
        for u in range(cols // 128):
            lanes = slice(u * 128, (u + 1) * 128)
            factor = 1.0 / (v - o_ref[:, lanes])
            for w in range(128 // TILE):
                row = t * (128 // TILE) + w
                keep = dm_ref[row:row + 1, lanes].astype(jnp.float32)
                inv[pl.ds(row * TILE, TILE), lanes] = factor[w * TILE:(w + 1) * TILE] * keep

    def receive(s, j):
        above, below = r + s + 1, r - s - 1

        late = (s, j) == (0, pieces - 1)

        @pl.when((above < R) & (r > 0) if late else above < R)
        def _():
            down(above, s, j).wait_recv()

            if s < R - 2:
                @pl.when(r > 0)
                def _():
                    down(above, s + 1, j).start()

        if s == 0 and not late:
            @pl.when(r == 0)
            def _():
                if j == 0:
                    domains().wait_recv()
                mask(1, j * tall, (j + 1) * tall, dm_above)

        @pl.when(below >= 0)
        def _():
            up(below, s, j).wait_recv()

            if s < R - 2:
                @pl.when(r < R - 1)
                def _():
                    up(below, s + 1, j).start()

    def product(block, j):
        return jnp.dot(a_all[block * parts + j], b_all[block, pl.ds(j * width, width), :],
                       preferred_element_type=jnp.float32)

    def add(s, j):
        @pl.when(r + s + 1 < R)
        def _():
            acc[...] += product(r + s + 1, j)

        @pl.when(r - s - 1 >= 0)
        def _():
            acc[...] += product(r - s - 1, j)

    strips = [(s, j) for s in range(R - 2) for j in range(pieces)]

    def take(count):
        for _ in range(min(count, len(strips))):
            receive(*strips.pop(0))

    near = [d for d in range(1, C) if d in bits]
    take(FIRST * SPLIT)
    for h in (1, 0):
        for d in near:
            arrives(d, h if 2 * d < C else 1 - h)
        if h:
            @pl.when(helper)
            def _():
                for core in range(2):
                    lend(core).wait_recv()
                    pass_on(core).start()
        take(SPLIT)
    for d in sorted(range(1, C), key=lambda d: d.bit_count()):
        if d not in near:
            for h in range(2):
                arrives(d, h)
    take(len(strips))

    @pl.when(r == 0)
    def _():
        down(1, 0, pieces - 1).wait_recv()
        mask(1, (pieces - 1) * tall, depth, dm_above)

    await_blocks(C, sib_recv)

    acc[...] = product(r, 0)
    for j in range(1, parts):
        acc[...] += product(r, j)
    for s in range(R - 2):
        for j in range(parts):
            add(s, j)

    def most(block):
        for j in range(parts - 1):
            acc[...] += product(block, j)
        k = (parts - 1) * width
        if SPLIT > 1:
            acc[...] += jnp.dot(a_all[block * parts + parts - 1, :, :width - tall], b_all[block, k:depth - tall, :],
                                preferred_element_type=jnp.float32)

    def strips_of(block):
        return b_all.at[block, pl.ds(0, depth - tall)]

    @pl.when(r == 0)
    def _():
        pltpu.make_async_copy(strips_of(R - 1), strips_of(R - 1), b_recv.at[place[0, R - 2, 0]]).wait()
        most(R - 1)

    @pl.when(r == R - 1)
    def _():
        pltpu.make_async_copy(strips_of(0), strips_of(0), b_recv.at[place[1, R - 2, 0]]).wait()
        most(0)

    await_blocks(2 * C - 1, a_sent)

    @pl.when((r == 0) | (r == R - 1))
    def _():
        await_blocks(1, b_sent)

    receive(R - 2, pieces - 1)

    def finish(block):
        k = (pieces - 1) * tall
        last = jnp.dot(a_all[block * parts + parts - 1, :, width - tall:], b_all[block, k:k + tall, :],
                       preferred_element_type=jnp.float32)
        acc[...] = (acc[...] + last) * inv[...]

    @pl.when(r == 0)
    def _():
        finish(R - 1)

    @pl.when(r == R - 1)
    def _():
        finish(0)

    @pl.when((r > 0) & (r < R - 1))
    def _():
        acc[...] = acc[...] * inv[...]
        await_blocks(R + 1, b_sent)

    @pl.when(r == 1)
    def _():
        domains().wait_send()

    @pl.when(helper)
    def _():
        pltpu.make_async_copy(lent, lent, load_sem.at[1]).wait()


def solution(mesh):
    R, C = mesh.shape["row"], mesh.shape["col"]

    def local(integrals, int_mask, amplitudes, domain_mask, virt_energy, occ_energy):
        rows, width = integrals.shape
        depth, cols = amplitudes.shape
        pieces = depth // width * SPLIT
        hbm = pl.BlockSpec(memory_space=pl.ANY)
        dma = pltpu.SemaphoreType.DMA
        operands = (integrals, int_mask.T, amplitudes, domain_mask,
                    virt_energy.reshape(1, rows), occ_energy.reshape(1, cols))
        return pl.pallas_call(
            functools.partial(kernel, R, C),
            out_shape=pltpu.VMEM((rows, cols), jnp.float32),
            in_specs=[hbm] * 6,
            out_specs=pl.BlockSpec(memory_space=pltpu.VMEM),
            scratch_shapes=[
                pltpu.VMEM((C * 2, rows, width), jnp.bfloat16),
                pltpu.VMEM((R, depth, cols), jnp.bfloat16),
                pltpu.VMEM((rows, cols), jnp.float32),
                pltpu.VMEM(int_mask.shape[::-1], jnp.int32),
                pltpu.VMEM(domain_mask.shape, jnp.int32),
                pltpu.VMEM(domain_mask.shape, jnp.int32),
                pltpu.VMEM((1, rows), jnp.float32),
                pltpu.VMEM((1, cols), jnp.float32),
                pltpu.VMEM((2, LENT, cols), jnp.bfloat16),
                dma((6,)), dma, dma((C, 2)), dma, dma, dma((arrivals(R, pieces)[1],)), dma,
                pltpu.SemaphoreType.REGULAR, pltpu.SemaphoreType.REGULAR,
            ],
            compiler_params=pltpu.CompilerParams(
                collective_id=0, has_side_effects=True, vmem_limit_bytes=32 * 2**20),
            cost_estimate=pl.CostEstimate(
                flops=2 * rows * depth * R * cols, bytes_accessed=4 * 2**20, transcendentals=0),
        )(*[pltpu.with_memory_space_constraint(x, pltpu.HBM) for x in operands])

    placed = (
        P("row", ("col", "pair")),
        P("row", ("col", "pair")),
        P("row", ("col", "pair")),
        P("row", ("col", "pair")),
        P("row"),
        P(("col", "pair")),
    )
    return jax.shard_map(
        local, mesh=mesh, in_specs=placed, out_specs=P("row", ("col", "pair")), check_vma=False
    )
```

```python
import functools

import jax
import jax.numpy as jnp
from jax import lax
from jax.experimental import pallas as pl
from jax.experimental.pallas import tpu as pltpu
from jax.sharding import PartitionSpec as P

TILE = 64
STRIPS = 4
LENT = (96, 32)
HELPER = 3
LAG = 2
MESH = pl.DeviceIdType.MESH


def flipped(index, distance, count):
    out, bit = 0, 1
    while bit < count:
        have = lax.rem(index // bit, 2)
        out = out + bit * (1 - have if (distance // bit) % 2 else have)
        bit *= 2
    return out


def passes(C, d, h):
    bits = [1 << i for i in range(C.bit_length() - 1)]
    low, high = d & -d, 1 << (d.bit_length() - 1)
    return [e for e in bits if d == 0 or (e < low if h == 0 else e > high)]


def arrivals(R):
    place, count = {}, 0
    for s in range(R - 1):
        own = list(range(STRIPS)) if s < R - 2 else [0] * (STRIPS - 1) + [1]
        for upward in (0, 1):
            if upward and 2 * s + 2 > R - 1:
                count -= own[-1] + 1
            for j in range(STRIPS):
                place[upward, s, j] = count + own[j]
            count += own[-1] + 1
    return place, count


def kernel(R, C, a_hbm, im_hbm, b_hbm, dm_hbm, v_hbm, o_hbm, acc,
           a_all, b_all, inv, im_ref, dm_ref, dm_above, energy,
           lent, load_sem, a_sent, a_recv, lent_in, sib_recv, b_sent, b_recv, dm_recv, above_in, plane_in):
    r, c, p = lax.axis_index("row"), lax.axis_index("col"), lax.axis_index("pair")
    q = 1 - p
    me = c * 2 + p
    rows, width = a_hbm.shape
    depth, cols = b_hbm.shape
    parts = depth // width
    tall = depth // 4
    spans = [pl.ds(j * tall, tall) for j in range(STRIPS)]
    last = STRIPS - 1
    half = rows // 2
    place, _ = arrivals(R)
    v_ref, o_ref = energy.at[:, pl.ds(0, rows)], energy.at[:, pl.ds(rows, cols)]
    bits = [1 << i for i in range(C.bit_length() - 1)]
    others = [flipped(c, d, C) for d in range(C)]
    giver = (r == 1) & (c == 0)
    helper = (r == 1) & (c == HELPER) & (p == 1)

    loads = [
        pltpu.make_async_copy(src, dst, load_sem.at[min(i, 4)]) for i, (src, dst) in enumerate([
            (dm_hbm, dm_ref), (b_hbm, b_all.at[r]), (im_hbm, im_ref), (a_hbm, a_all.at[me]),
            (v_hbm, v_ref), (o_hbm, o_ref)])
    ]

    barrier = pltpu.get_barrier_semaphore()

    def greet(device):
        pl.semaphore_signal(barrier, inc=1, device_id=device, device_id_type=MESH)

    @pl.when(r < R - 1)
    def _():
        greet((r + 1, c, p))

    @pl.when(p == 1)
    def _():
        for e in bits:
            greet((r, others[e], p))

    @pl.when(p == 0)
    def _():
        greet((r, c, q))

    for load in loads:
        load.start()

    @pl.when(p == 1)
    def _():
        pl.semaphore_wait(barrier, (r + R - 1) // R + len(bits) + 1)

    @pl.when((p == 0) & (r > 0))
    def _():
        pl.semaphore_wait(barrier, 1)

    def strip(block, j):
        return b_all.at[block, spans[j]]

    def down(block, s, j):
        return pltpu.make_async_remote_copy(
            src_ref=strip(block, j), dst_ref=strip(block, j),
            send_sem=b_sent, recv_sem=b_recv.at[place[0, s, j]],
            device_id=(r - 1, c, p), device_id_type=MESH)

    def up(block, s, j):
        return pltpu.make_async_remote_copy(
            src_ref=strip(block, j), dst_ref=strip(block, j),
            send_sem=b_sent, recv_sem=b_recv.at[place[1, s, j]],
            device_id=(r + 1, c, p), device_id_type=MESH)

    def raw(j):
        return pltpu.make_async_remote_copy(
            src_ref=b_hbm.at[spans[j]], dst_ref=strip(r, j),
            send_sem=b_sent, recv_sem=b_recv.at[place[0, 0, j]],
            device_id=(r - 1, c, p), device_id_type=MESH)

    def cut(core):
        here = pl.ds(depth - tall, tall - LENT[core])
        return pltpu.make_async_remote_copy(
            src_ref=b_hbm.at[here], dst_ref=b_all.at[1, here],
            send_sem=b_sent, recv_sem=b_recv.at[place[0, 0, last]],
            device_id=(0, c, p), device_id_type=MESH)

    def lend(core):
        return pltpu.make_async_remote_copy(
            src_ref=b_hbm.at[pl.ds(depth - LENT[core], LENT[core])],
            dst_ref=lent.at[pl.ds(core * LENT[0], LENT[core])],
            send_sem=b_sent, recv_sem=lent_in,
            device_id=(1, HELPER, 1), device_id_type=MESH)

    def pass_on(core):
        return pltpu.make_async_remote_copy(
            src_ref=lent.at[pl.ds(core * LENT[0], LENT[core])],
            dst_ref=b_all.at[1, pl.ds(depth - LENT[core], LENT[core])],
            send_sem=load_sem.at[1], recv_sem=b_recv.at[place[0, 0, last]],
            device_id=(0, 0, core), device_id_type=MESH)

    def domains():
        return pltpu.make_async_remote_copy(
            src_ref=dm_ref, dst_ref=dm_above, send_sem=load_sem.at[0], recv_sem=dm_recv,
            device_id=(r - 1, c, p), device_id_type=MESH)

    def onward(d, h):
        return passes(C, d, h)

    relayed = [(d, h) for d in range(1, C) for h in range(2) if onward(d, h)]
    leaves = [(d, h) for d in range(1, C) for h in range(2) if not onward(d, h)]

    def halves(d, h):
        return 1 + relayed.index((d, h)) if onward(d, h) else 0

    def across(d, e, h):
        piece = a_all.at[others[d] * 2 + p, pl.ds(h * half, half)]
        return pltpu.make_async_remote_copy(
            src_ref=piece, dst_ref=piece,
            send_sem=a_sent, recv_sem=a_recv.at[halves(d + e, h)],
            device_id=(r, others[e], p), device_id_type=MESH)

    def sibling(d, h):
        piece = a_all.at[others[d] * 2 + p, pl.ds(h * half, half)]
        return pltpu.make_async_remote_copy(
            src_ref=piece, dst_ref=piece,
            send_sem=a_sent, recv_sem=sib_recv,
            device_id=(r, c, q), device_id_type=MESH)

    def await_blocks(count, sem):
        blocks = a_all.at[pl.ds(0, count)]
        pltpu.make_async_copy(blocks, blocks, sem).wait()

    def arrives(d, h):
        low, high = d & -d, 1 << (d.bit_length() - 1)
        e = low if h == 0 else high
        piece = a_all.at[others[d] * 2 + p, pl.ds(h * half, half)]
        pltpu.make_async_remote_copy(
            src_ref=piece, dst_ref=piece,
            send_sem=a_sent, recv_sem=a_recv.at[halves(d, h)],
            device_id=(r, others[e], p), device_id_type=MESH).wait_recv()
        for e in onward(d, h):
            across(d, e, h).start()
        sibling(d, h).start()

    def mask(block, j, domain):
        for t in range(spans[j].start // TILE, (spans[j].start + spans[j].size) // TILE):
            here = pl.ds(t * TILE, TILE)
            b_all[block, here, :] = b_all[block, here, :] * domain[t:t + 1, :].astype(jnp.bfloat16)

    @pl.when(r == 1)
    def _():
        for j in range(last):
            raw(j).start()

    for core in range(2):
        @pl.when(giver & (p == core))
        def _():
            cut(core).start()

    @pl.when((r == 1) & (c > 0))
    def _():
        raw(last).start()

    @pl.when(r > 0)
    def _():
        pl.semaphore_signal(above_in, inc=1, device_id=(r - 1, c, p), device_id_type=MESH)

    @pl.when(p == 1)
    def _():
        for e in bits:
            pl.semaphore_signal(plane_in, inc=1, device_id=(r, others[e], p), device_id_type=MESH)

    loads[0].wait()
    loads[1].wait()

    @pl.when(r == 1)
    def _():
        domains().start()

    for j in range(STRIPS):
        mask(r, j, dm_ref)

        @pl.when(r > 1)
        def _():
            down(r, 0, j).start()

    @pl.when(p == 1)
    def _():
        pl.semaphore_wait(plane_in, len(bits))
        pl.semaphore_signal(plane_in, inc=1, device_id=(r, c, q), device_id_type=MESH)

    def rise():
        @pl.when(r < R - 1)
        def _():
            pl.semaphore_wait(above_in, 1)
            for j in range(STRIPS):
                up(r, 0, j).start()

    @pl.when(p == 0)
    def _():
        rise()

    loads[2].wait()
    loads[3].wait()
    lane = lax.broadcasted_iota(jnp.int32, (1, width), 1) // TILE
    for t in range(rows // TILE):
        keep = jnp.zeros((1, width), jnp.float32)
        for u in range(width // TILE):
            keep = jnp.where(lane == u, im_ref[u:u + 1, t:t + 1].astype(jnp.float32), keep)
        here = pl.ds(t * TILE, TILE)
        a_all[me, here, :] = a_all[me, here, :] * keep.astype(jnp.bfloat16)

    @pl.when(p == 0)
    def _():
        pl.semaphore_wait(plane_in, 1)

    for core in range(2):
        @pl.when(giver & (p == core))
        def _():
            lend(core).start()

    for h in (1, 0):
        for e in bits:
            g = h if 2 * e < C else 1 - h
            across(0, e, g).start()
    for h in range(2):
        sibling(0, h).start()

    @pl.when(p == 1)
    def _():
        rise()

    pltpu.make_async_copy(energy, energy, load_sem.at[4]).wait()
    for t in range(rows // 128):
        v = jnp.broadcast_to(v_ref[:, t * 128:(t + 1) * 128], (128, 128)).T
        for u in range(cols // 128):
            lanes = slice(u * 128, (u + 1) * 128)
            factor = 1.0 / (v - o_ref[:, lanes])
            for w in range(128 // TILE):
                row = t * (128 // TILE) + w
                keep = dm_ref[row:row + 1, lanes].astype(jnp.float32)
                inv[pl.ds(row * TILE, TILE), lanes] = factor[w * TILE:(w + 1) * TILE] * keep

    def from_above(s, j):
        above = r + s + 1

        late = (s, j) == (0, last)

        @pl.when((above < R) & (r > 0) if late else above < R)
        def _():
            down(above, s, j).wait_recv()

            if s < R - 2:
                @pl.when(r > 0)
                def _():
                    down(above, s + 1, j).start()

        if s == 0 and not late:
            @pl.when(r == 0)
            def _():
                if j == 0:
                    domains().wait_recv()
                mask(1, j, dm_above)

    def from_below(s, j):
        below = r - s - 1

        @pl.when(below >= 0)
        def _():
            up(below, s, j).wait_recv()

            if s < R - 2:
                @pl.when(r < R - 1)
                def _():
                    up(below, s + 1, j).start()

    def product(block, j):
        return jnp.dot(a_all[block * parts + j], b_all[block, pl.ds(j * width, width), :],
                       preferred_element_type=jnp.float32)

    def add(s, j):
        @pl.when(r + s + 1 < R)
        def _():
            acc[...] += product(r + s + 1, j)

        @pl.when(r - s - 1 >= 0)
        def _():
            acc[...] += product(r - s - 1, j)

    each = [(s, j) for s in range(R - 2) for j in range(STRIPS)]
    strips = sorted([(i, from_above, *x) for i, x in enumerate(each)] + [(i + LAG, from_below, *x) for i, x in enumerate(each)],
                    key=lambda x: x[0])

    def take(count):
        for _ in range(min(count, len(strips))):
            _, take_from, s, j = strips.pop(0)
            take_from(s, j)

    order = sorted(relayed, key=lambda x: (x[0].bit_count(), x[1] if 2 * x[0] >= C else 1 - x[1]))
    take(6)
    for d, h in order:
        arrives(d, h)

    @pl.when(helper)
    def _():
        pltpu.make_async_copy(lent, lent, lent_in).wait()
        for core in range(2):
            pass_on(core).start()

    take(6)
    await_blocks(len(leaves) // 2, a_recv.at[0])
    for d, h in leaves:
        sibling(d, h).start()
    take(len(strips))

    @pl.when(r == 0)
    def _():
        down(1, 0, last).wait_recv()
        mask(1, last, dm_above)

    await_blocks(C, sib_recv)

    acc[...] = product(r, 0)
    for j in range(1, parts):
        acc[...] += product(r, j)
    for s in range(R - 2):
        for j in range(parts):
            add(s, j)

    def most(block):
        for j in range(parts - 1):
            acc[...] += product(block, j)
        k = (parts - 1) * width
        if tall < width:
            acc[...] += jnp.dot(a_all[block * parts + parts - 1, :, :width - tall], b_all[block, k:depth - tall, :],
                                preferred_element_type=jnp.float32)

    def strips_of(block):
        return b_all.at[block, pl.ds(0, depth - tall)]

    @pl.when(r == 0)
    def _():
        pltpu.make_async_copy(strips_of(R - 1), strips_of(R - 1), b_recv.at[place[0, R - 2, 0]]).wait()
        most(R - 1)

    @pl.when(r == R - 1)
    def _():
        pltpu.make_async_copy(strips_of(0), strips_of(0), b_recv.at[place[1, R - 2, 0]]).wait()
        most(0)

    await_blocks(2 * C - 1, a_sent)

    @pl.when((r == 0) | (r == R - 1))
    def _():
        await_blocks(1, b_sent)

    from_above(R - 2, last)
    from_below(R - 2, last)

    def finish(block):
        k = depth - tall
        term = jnp.dot(a_all[block * parts + parts - 1, :, width - tall:], b_all[block, k:k + tall, :],
                       preferred_element_type=jnp.float32)
        acc[...] = (acc[...] + term) * inv[...]

    @pl.when(r == 0)
    def _():
        finish(R - 1)

    @pl.when(r == R - 1)
    def _():
        finish(0)

    @pl.when((r > 0) & (r < R - 1))
    def _():
        acc[...] = acc[...] * inv[...]
        await_blocks(R + 1, b_sent)

    @pl.when(r == 1)
    def _():
        domains().wait_send()

    @pl.when(helper)
    def _():
        pltpu.make_async_copy(lent, lent, load_sem.at[1]).wait()


def solution(mesh):
    R, C = mesh.shape["row"], mesh.shape["col"]

    def local(integrals, int_mask, amplitudes, domain_mask, virt_energy, occ_energy):
        rows, width = integrals.shape
        depth, cols = amplitudes.shape
        hbm = pl.BlockSpec(memory_space=pl.ANY)
        dma = pltpu.SemaphoreType.DMA
        relays = sum(bool(passes(C, d, h)) for d in range(1, C) for h in range(2))
        operands = (integrals, int_mask.T, amplitudes, domain_mask,
                    virt_energy.reshape(1, rows), occ_energy.reshape(1, cols))
        return pl.pallas_call(
            functools.partial(kernel, R, C),
            out_shape=pltpu.VMEM((rows, cols), jnp.float32),
            in_specs=[hbm] * 6,
            out_specs=pl.BlockSpec(memory_space=pltpu.VMEM),
            scratch_shapes=[
                pltpu.VMEM((C * 2, rows, width), jnp.bfloat16),
                pltpu.VMEM((R, depth, cols), jnp.bfloat16),
                pltpu.VMEM((rows, cols), jnp.float32),
                pltpu.VMEM(int_mask.shape[::-1], jnp.int32),
                pltpu.VMEM(domain_mask.shape, jnp.int32),
                pltpu.VMEM(domain_mask.shape, jnp.int32),
                pltpu.VMEM((1, rows + cols), jnp.float32),
                pltpu.VMEM((sum(LENT), cols), jnp.bfloat16),
                dma((5,)), dma, dma((1 + relays,)), dma, dma, dma, dma((arrivals(R)[1],)), dma,
                pltpu.SemaphoreType.REGULAR, pltpu.SemaphoreType.REGULAR,
            ],
            compiler_params=pltpu.CompilerParams(
                collective_id=0, has_side_effects=True, vmem_limit_bytes=32 * 2**20),
            cost_estimate=pl.CostEstimate(
                flops=2 * rows * depth * R * cols, bytes_accessed=4 * 2**20, transcendentals=0),
        )(*[pltpu.with_memory_space_constraint(x, pltpu.HBM) for x in operands])

    placed = (
        P("row", ("col", "pair")),
        P("row", ("col", "pair")),
        P("row", ("col", "pair")),
        P("row", ("col", "pair")),
        P("row"),
        P(("col", "pair")),
    )
    return jax.shard_map(
        local, mesh=mesh, in_specs=placed, out_specs=P("row", ("col", "pair")), check_vma=False
    )
```

```python
import functools

import jax
import jax.numpy as jnp
from jax import lax
from jax.experimental import pallas as pl
from jax.experimental.pallas import tpu as pltpu
from jax.sharding import PartitionSpec as P

TILE = 64
STRIPS = 4
LENT = (112, 48)
HELPERS = (3, 2)
LAG = 2
MESH = pl.DeviceIdType.MESH


def flipped(index, distance, count):
    out, bit = 0, 1
    while bit < count:
        have = lax.rem(index // bit, 2)
        out = out + bit * (1 - have if (distance // bit) % 2 else have)
        bit *= 2
    return out


def passes(C, d, h):
    bits = [1 << i for i in range(C.bit_length() - 1)]
    low, high = d & -d, 1 << (d.bit_length() - 1)
    return [e for e in bits if d == 0 or (e < low if h == 0 else e > high)]


def arrivals(R):
    place, count = {}, 0
    for s in range(R - 1):
        own = list(range(STRIPS)) if s < R - 2 else [0] * (STRIPS - 1) + [1]
        for upward in (0, 1):
            if upward and 2 * s + 2 > R - 1:
                count -= own[-1] + 1
            for j in range(STRIPS):
                place[upward, s, j] = count + own[j]
            count += own[-1] + 1
    return place, count


def kernel(R, C, a_hbm, im_hbm, b_hbm, dm_hbm, v_hbm, o_hbm, acc,
           a_all, b_all, inv, im_ref, dm_ref, dm_above, energy,
           lent, load_sem, a_sent, a_recv, lent_in, sib_recv, b_sent, b_recv, dm_recv, above_in, plane_in):
    r, c, p = lax.axis_index("row"), lax.axis_index("col"), lax.axis_index("pair")
    q = 1 - p
    me = c * 2 + p
    rows, width = a_hbm.shape
    depth, cols = b_hbm.shape
    parts = depth // width
    tall = depth // 4
    spans = [pl.ds(j * tall, tall) for j in range(STRIPS)]
    last = STRIPS - 1
    half = rows // 2
    place, _ = arrivals(R)
    v_ref, o_ref = energy.at[:, pl.ds(0, rows)], energy.at[:, pl.ds(rows, cols)]
    bits = [1 << i for i in range(C.bit_length() - 1)]
    others = [flipped(c, d, C) for d in range(C)]
    giver = (r == 1) & (c == 0)
    helper = [(r == 1) & (c == HELPERS[core]) & (p == 1 - core) for core in range(2)]

    loads = [
        pltpu.make_async_copy(src, dst, load_sem.at[min(i, 4)]) for i, (src, dst) in enumerate([
            (dm_hbm, dm_ref), (b_hbm, b_all.at[r]), (im_hbm, im_ref), (a_hbm, a_all.at[me]),
            (v_hbm, v_ref), (o_hbm, o_ref)])
    ]

    barrier = pltpu.get_barrier_semaphore()

    def greet(device):
        pl.semaphore_signal(barrier, inc=1, device_id=device, device_id_type=MESH)

    @pl.when(r < R - 1)
    def _():
        greet((r + 1, c, p))

    @pl.when(p == 1)
    def _():
        for e in bits:
            greet((r, others[e], p))

    @pl.when(p == 0)
    def _():
        greet((r, c, q))

    for load in loads:
        load.start()

    @pl.when(p == 1)
    def _():
        pl.semaphore_wait(barrier, (r + R - 1) // R + len(bits) + 1)

    @pl.when((p == 0) & (r > 0))
    def _():
        pl.semaphore_wait(barrier, 1)

    def strip(block, j):
        return b_all.at[block, spans[j]]

    def down(block, s, j):
        return pltpu.make_async_remote_copy(
            src_ref=strip(block, j), dst_ref=strip(block, j),
            send_sem=b_sent, recv_sem=b_recv.at[place[0, s, j]],
            device_id=(r - 1, c, p), device_id_type=MESH)

    def up(block, s, j):
        return pltpu.make_async_remote_copy(
            src_ref=strip(block, j), dst_ref=strip(block, j),
            send_sem=b_sent, recv_sem=b_recv.at[place[1, s, j]],
            device_id=(r + 1, c, p), device_id_type=MESH)

    def raw(j):
        return pltpu.make_async_remote_copy(
            src_ref=b_hbm.at[spans[j]], dst_ref=strip(r, j),
            send_sem=b_sent, recv_sem=b_recv.at[place[0, 0, j]],
            device_id=(r - 1, c, p), device_id_type=MESH)

    def cut(core):
        here = pl.ds(depth - tall, tall - LENT[core])
        return pltpu.make_async_remote_copy(
            src_ref=b_hbm.at[here], dst_ref=b_all.at[1, here],
            send_sem=b_sent, recv_sem=b_recv.at[place[0, 0, last]],
            device_id=(0, c, p), device_id_type=MESH)

    def lend(core):
        return pltpu.make_async_remote_copy(
            src_ref=b_hbm.at[pl.ds(depth - LENT[core], LENT[core])],
            dst_ref=lent.at[pl.ds(core * LENT[0], LENT[core])],
            send_sem=b_sent, recv_sem=lent_in,
            device_id=(1, HELPERS[core], 1 - core), device_id_type=MESH)

    def pass_on(core):
        return pltpu.make_async_remote_copy(
            src_ref=lent.at[pl.ds(core * LENT[0], LENT[core])],
            dst_ref=b_all.at[1, pl.ds(depth - LENT[core], LENT[core])],
            send_sem=load_sem.at[1], recv_sem=b_recv.at[place[0, 0, last]],
            device_id=(0, 0, core), device_id_type=MESH)

    def domains():
        return pltpu.make_async_remote_copy(
            src_ref=dm_ref, dst_ref=dm_above, send_sem=load_sem.at[0], recv_sem=dm_recv,
            device_id=(r - 1, c, p), device_id_type=MESH)

    def onward(d, h):
        return passes(C, d, h)

    relayed = [(d, h) for d in range(1, C) for h in range(2) if onward(d, h)]
    leaves = [(d, h) for d in range(1, C) for h in range(2) if not onward(d, h)]

    def halves(d, h):
        return 1 + relayed.index((d, h)) if onward(d, h) else 0

    def across(d, e, h):
        piece = a_all.at[others[d] * 2 + p, pl.ds(h * half, half)]
        return pltpu.make_async_remote_copy(
            src_ref=piece, dst_ref=piece,
            send_sem=a_sent, recv_sem=a_recv.at[halves(d + e, h)],
            device_id=(r, others[e], p), device_id_type=MESH)

    def sibling(d, h):
        piece = a_all.at[others[d] * 2 + p, pl.ds(h * half, half)]
        return pltpu.make_async_remote_copy(
            src_ref=piece, dst_ref=piece,
            send_sem=a_sent, recv_sem=sib_recv,
            device_id=(r, c, q), device_id_type=MESH)

    def await_blocks(count, sem):
        blocks = a_all.at[pl.ds(0, count)]
        pltpu.make_async_copy(blocks, blocks, sem).wait()

    def arrives(d, h):
        low, high = d & -d, 1 << (d.bit_length() - 1)
        e = low if h == 0 else high
        piece = a_all.at[others[d] * 2 + p, pl.ds(h * half, half)]
        pltpu.make_async_remote_copy(
            src_ref=piece, dst_ref=piece,
            send_sem=a_sent, recv_sem=a_recv.at[halves(d, h)],
            device_id=(r, others[e], p), device_id_type=MESH).wait_recv()
        for e in onward(d, h):
            across(d, e, h).start()
        sibling(d, h).start()

    def mask(block, j, domain):
        for t in range(spans[j].start // TILE, (spans[j].start + spans[j].size) // TILE):
            here = pl.ds(t * TILE, TILE)
            b_all[block, here, :] = b_all[block, here, :] * domain[t:t + 1, :].astype(jnp.bfloat16)

    @pl.when(r == 1)
    def _():
        for j in range(last):
            raw(j).start()

    for core in range(2):
        @pl.when(giver & (p == core))
        def _():
            cut(core).start()

    @pl.when((r == 1) & (c > 0))
    def _():
        raw(last).start()

    @pl.when(r > 0)
    def _():
        pl.semaphore_signal(above_in, inc=1, device_id=(r - 1, c, p), device_id_type=MESH)

    @pl.when(p == 1)
    def _():
        for e in bits:
            pl.semaphore_signal(plane_in, inc=1, device_id=(r, others[e], p), device_id_type=MESH)

    loads[0].wait()
    loads[1].wait()

    @pl.when(r == 1)
    def _():
        domains().start()

    for j in range(STRIPS):
        mask(r, j, dm_ref)

        @pl.when(r > 1)
        def _():
            down(r, 0, j).start()

    @pl.when(p == 1)
    def _():
        pl.semaphore_wait(plane_in, len(bits))
        pl.semaphore_signal(plane_in, inc=1, device_id=(r, c, q), device_id_type=MESH)

    def rise():
        @pl.when(r < R - 1)
        def _():
            pl.semaphore_wait(above_in, 1)
            for j in range(STRIPS):
                up(r, 0, j).start()

    @pl.when(p == 0)
    def _():
        rise()

    loads[2].wait()
    loads[3].wait()
    lane = lax.broadcasted_iota(jnp.int32, (1, width), 1) // TILE
    for t in range(rows // TILE):
        keep = jnp.zeros((1, width), jnp.float32)
        for u in range(width // TILE):
            keep = jnp.where(lane == u, im_ref[u:u + 1, t:t + 1].astype(jnp.float32), keep)
        here = pl.ds(t * TILE, TILE)
        a_all[me, here, :] = a_all[me, here, :] * keep.astype(jnp.bfloat16)

    @pl.when(p == 0)
    def _():
        pl.semaphore_wait(plane_in, 1)

    for core in range(2):
        @pl.when(giver & (p == core))
        def _():
            lend(core).start()

    for h in (1, 0):
        for e in bits:
            g = h if 2 * e < C else 1 - h
            across(0, e, g).start()
    for h in range(2):
        sibling(0, h).start()

    @pl.when(p == 1)
    def _():
        rise()

    pltpu.make_async_copy(energy, energy, load_sem.at[4]).wait()
    for t in range(rows // 128):
        v = jnp.broadcast_to(v_ref[:, t * 128:(t + 1) * 128], (128, 128)).T
        for u in range(cols // 128):
            lanes = slice(u * 128, (u + 1) * 128)
            factor = 1.0 / (v - o_ref[:, lanes])
            for w in range(128 // TILE):
                row = t * (128 // TILE) + w
                keep = dm_ref[row:row + 1, lanes].astype(jnp.float32)
                inv[pl.ds(row * TILE, TILE), lanes] = factor[w * TILE:(w + 1) * TILE] * keep

    def from_above(s, j):
        above = r + s + 1

        late = (s, j) == (0, last)

        @pl.when((above < R) & (r > 0) if late else above < R)
        def _():
            down(above, s, j).wait_recv()

            if s < R - 2:
                @pl.when(r > 0)
                def _():
                    down(above, s + 1, j).start()

        if s == 0 and not late:
            @pl.when(r == 0)
            def _():
                if j == 0:
                    domains().wait_recv()
                mask(1, j, dm_above)

    def from_below(s, j):
        below = r - s - 1

        @pl.when(below >= 0)
        def _():
            up(below, s, j).wait_recv()

            if s < R - 2:
                @pl.when(r < R - 1)
                def _():
                    up(below, s + 1, j).start()

    def product(block, j):
        return jnp.dot(a_all[block * parts + j], b_all[block, pl.ds(j * width, width), :],
                       preferred_element_type=jnp.float32)

    def add(s, j):
        @pl.when(r + s + 1 < R)
        def _():
            acc[...] += product(r + s + 1, j)

        @pl.when(r - s - 1 >= 0)
        def _():
            acc[...] += product(r - s - 1, j)

    each = [(s, j) for s in range(R - 2) for j in range(STRIPS)]
    strips = sorted([(i, from_above, *x) for i, x in enumerate(each)] + [(i + LAG, from_below, *x) for i, x in enumerate(each)],
                    key=lambda x: x[0])

    def take(count):
        for _ in range(min(count, len(strips))):
            _, take_from, s, j = strips.pop(0)
            take_from(s, j)

    order = sorted(relayed, key=lambda x: (x[0].bit_count(), x[1] if 2 * x[0] >= C else 1 - x[1]))
    take(6)
    for d, h in order:
        arrives(d, h)

    for core in range(2):
        @pl.when(helper[core])
        def _():
            lend(core).wait_recv()
            pass_on(core).start()

    take(6)
    await_blocks(len(leaves) // 2, a_recv.at[0])
    for d, h in leaves:
        sibling(d, h).start()
    take(len(strips))

    @pl.when(r == 0)
    def _():
        down(1, 0, last).wait_recv()
        mask(1, last, dm_above)

    await_blocks(C, sib_recv)

    acc[...] = product(r, 0)
    for j in range(1, parts):
        acc[...] += product(r, j)
    for s in range(R - 2):
        for j in range(parts):
            add(s, j)

    def most(block):
        for j in range(parts - 1):
            acc[...] += product(block, j)
        k = (parts - 1) * width
        if tall < width:
            acc[...] += jnp.dot(a_all[block * parts + parts - 1, :, :width - tall], b_all[block, k:depth - tall, :],
                                preferred_element_type=jnp.float32)

    def strips_of(block):
        return b_all.at[block, pl.ds(0, depth - tall)]

    @pl.when(r == 0)
    def _():
        pltpu.make_async_copy(strips_of(R - 1), strips_of(R - 1), b_recv.at[place[0, R - 2, 0]]).wait()
        most(R - 1)

    @pl.when(r == R - 1)
    def _():
        pltpu.make_async_copy(strips_of(0), strips_of(0), b_recv.at[place[1, R - 2, 0]]).wait()
        most(0)

    await_blocks(2 * C - 1, a_sent)

    @pl.when((r == 0) | (r == R - 1))
    def _():
        await_blocks(1, b_sent)

    from_above(R - 2, last)
    from_below(R - 2, last)

    def finish(block):
        k = depth - tall
        term = jnp.dot(a_all[block * parts + parts - 1, :, width - tall:], b_all[block, k:k + tall, :],
                       preferred_element_type=jnp.float32)
        acc[...] = (acc[...] + term) * inv[...]

    @pl.when(r == 0)
    def _():
        finish(R - 1)

    @pl.when(r == R - 1)
    def _():
        finish(0)

    @pl.when((r > 0) & (r < R - 1))
    def _():
        acc[...] = acc[...] * inv[...]
        await_blocks(R + 1, b_sent)

    @pl.when(r == 1)
    def _():
        domains().wait_send()

    for core in range(2):
        @pl.when(helper[core])
        def _():
            pass_on(core).wait_send()


def solution(mesh):
    R, C = mesh.shape["row"], mesh.shape["col"]

    def local(integrals, int_mask, amplitudes, domain_mask, virt_energy, occ_energy):
        rows, width = integrals.shape
        depth, cols = amplitudes.shape
        hbm = pl.BlockSpec(memory_space=pl.ANY)
        dma = pltpu.SemaphoreType.DMA
        relays = sum(bool(passes(C, d, h)) for d in range(1, C) for h in range(2))
        operands = (integrals, int_mask.T, amplitudes, domain_mask,
                    virt_energy.reshape(1, rows), occ_energy.reshape(1, cols))
        return pl.pallas_call(
            functools.partial(kernel, R, C),
            out_shape=pltpu.VMEM((rows, cols), jnp.float32),
            in_specs=[hbm] * 6,
            out_specs=pl.BlockSpec(memory_space=pltpu.VMEM),
            scratch_shapes=[
                pltpu.VMEM((C * 2, rows, width), jnp.bfloat16),
                pltpu.VMEM((R, depth, cols), jnp.bfloat16),
                pltpu.VMEM((rows, cols), jnp.float32),
                pltpu.VMEM(int_mask.shape[::-1], jnp.int32),
                pltpu.VMEM(domain_mask.shape, jnp.int32),
                pltpu.VMEM(domain_mask.shape, jnp.int32),
                pltpu.VMEM((1, rows + cols), jnp.float32),
                pltpu.VMEM((sum(LENT), cols), jnp.bfloat16),
                dma((5,)), dma, dma((1 + relays,)), dma, dma, dma, dma((arrivals(R)[1],)), dma,
                pltpu.SemaphoreType.REGULAR, pltpu.SemaphoreType.REGULAR,
            ],
            compiler_params=pltpu.CompilerParams(
                collective_id=0, has_side_effects=True, vmem_limit_bytes=32 * 2**20),
            cost_estimate=pl.CostEstimate(
                flops=2 * rows * depth * R * cols, bytes_accessed=4 * 2**20, transcendentals=0),
        )(*[pltpu.with_memory_space_constraint(x, pltpu.HBM) for x in operands])

    placed = (
        P("row", ("col", "pair")),
        P("row", ("col", "pair")),
        P("row", ("col", "pair")),
        P("row", ("col", "pair")),
        P("row"),
        P(("col", "pair")),
    )
    return jax.shard_map(
        local, mesh=mesh, in_specs=placed, out_specs=P("row", ("col", "pair")), check_vma=False
    )
```

```python
import functools

import jax
import jax.numpy as jnp
from jax import lax
from jax.experimental import pallas as pl
from jax.experimental.pallas import tpu as pltpu
from jax.sharding import PartitionSpec as P

TILE = 64
STRIPS = 4
LENT = (112, 48)
HELPERS = (3, 2)
LAG = 2
MESH = pl.DeviceIdType.MESH


def flipped(index, distance, count):
    out, bit = 0, 1
    while bit < count:
        have = lax.rem(index // bit, 2)
        out = out + bit * (1 - have if (distance // bit) % 2 else have)
        bit *= 2
    return out


def passes(C, d, h):
    bits = [1 << i for i in range(C.bit_length() - 1)]
    low, high = d & -d, 1 << (d.bit_length() - 1)
    return [e for e in bits if d == 0 or (e < low if h == 0 else e > high)]


def arrivals(R):
    place, count = {}, 0
    for s in range(R - 1):
        own = list(range(STRIPS)) if s < R - 2 else [0] * (STRIPS - 1) + [1]
        for upward in (0, 1):
            if upward and 2 * s + 2 > R - 1:
                count -= own[-1] + 1
            for j in range(STRIPS):
                place[upward, s, j] = count + own[j]
            count += own[-1] + 1
    return place, count


def kernel(R, C, a_hbm, im_hbm, b_hbm, dm_hbm, v_hbm, o_hbm, acc,
           a_all, b_all, inv, im_ref, dm_ref, dm_above, energy,
           lent, load_sem, a_recv, lent_in, sib_recv, b_sent, b_recv, dm_recv, above_in, plane_in):
    r, c, p = lax.axis_index("row"), lax.axis_index("col"), lax.axis_index("pair")
    q = 1 - p
    me = c * 2 + p
    rows, width = a_hbm.shape
    depth, cols = b_hbm.shape
    parts = depth // width
    tall = depth // 4
    spans = [pl.ds(j * tall, tall) for j in range(STRIPS)]
    last = STRIPS - 1
    half = rows // 2
    place, _ = arrivals(R)
    v_ref, o_ref = energy.at[:, pl.ds(0, rows)], energy.at[:, pl.ds(rows, cols)]
    bits = [1 << i for i in range(C.bit_length() - 1)]
    others = [flipped(c, d, C) for d in range(C)]
    giver = (r == 1) & (c == 0)
    helper = [(r == 1) & (c == HELPERS[core]) & (p == 1 - core) for core in range(2)]

    loads = [
        pltpu.make_async_copy(src, dst, load_sem.at[min(i, 4)]) for i, (src, dst) in enumerate([
            (dm_hbm, dm_ref), (b_hbm, b_all.at[r]), (im_hbm, im_ref), (a_hbm, a_all.at[me]),
            (v_hbm, v_ref), (o_hbm, o_ref)])
    ]

    barrier = pltpu.get_barrier_semaphore()

    def greet(device):
        pl.semaphore_signal(barrier, inc=1, device_id=device, device_id_type=MESH)

    @pl.when(r < R - 1)
    def _():
        greet((r + 1, c, p))

    @pl.when(p == 1)
    def _():
        for e in bits:
            greet((r, others[e], p))

    @pl.when(p == 0)
    def _():
        greet((r, c, q))

    for load in loads:
        load.start()

    @pl.when(p == 1)
    def _():
        pl.semaphore_wait(barrier, (r + R - 1) // R + len(bits) + 1)

    @pl.when((p == 0) & (r > 0))
    def _():
        pl.semaphore_wait(barrier, 1)

    def strip(block, j):
        return b_all.at[block, spans[j]]

    def down(block, s, j):
        return pltpu.make_async_remote_copy(
            src_ref=strip(block, j), dst_ref=strip(block, j),
            send_sem=b_sent, recv_sem=b_recv.at[place[0, s, j]],
            device_id=(r - 1, c, p), device_id_type=MESH)

    def up(block, s, j):
        return pltpu.make_async_remote_copy(
            src_ref=strip(block, j), dst_ref=strip(block, j),
            send_sem=b_sent, recv_sem=b_recv.at[place[1, s, j]],
            device_id=(r + 1, c, p), device_id_type=MESH)

    def raw(j):
        return pltpu.make_async_remote_copy(
            src_ref=b_hbm.at[spans[j]], dst_ref=strip(r, j),
            send_sem=b_sent, recv_sem=b_recv.at[place[0, 0, j]],
            device_id=(r - 1, c, p), device_id_type=MESH)

    def cut(core):
        here = pl.ds(depth - tall, tall - LENT[core])
        return pltpu.make_async_remote_copy(
            src_ref=b_hbm.at[here], dst_ref=b_all.at[1, here],
            send_sem=b_sent, recv_sem=b_recv.at[place[0, 0, last]],
            device_id=(0, c, p), device_id_type=MESH)

    def lend(core):
        return pltpu.make_async_remote_copy(
            src_ref=b_hbm.at[pl.ds(depth - LENT[core], LENT[core])],
            dst_ref=lent.at[pl.ds(core * LENT[0], LENT[core])],
            send_sem=b_sent, recv_sem=lent_in,
            device_id=(1, HELPERS[core], 1 - core), device_id_type=MESH)

    def pass_on(core):
        return pltpu.make_async_remote_copy(
            src_ref=lent.at[pl.ds(core * LENT[0], LENT[core])],
            dst_ref=b_all.at[1, pl.ds(depth - LENT[core], LENT[core])],
            send_sem=load_sem.at[1], recv_sem=b_recv.at[place[0, 0, last]],
            device_id=(0, 0, core), device_id_type=MESH)

    def domains():
        return pltpu.make_async_remote_copy(
            src_ref=dm_ref, dst_ref=dm_above, send_sem=load_sem.at[0], recv_sem=dm_recv,
            device_id=(r - 1, c, p), device_id_type=MESH)

    def onward(d, h):
        return passes(C, d, h)

    relayed = [(d, h) for d in range(1, C) for h in range(2) if onward(d, h)]
    leaves = [(d, h) for d in range(1, C) for h in range(2) if not onward(d, h)]

    def halves(d, h):
        return 1 + relayed.index((d, h)) if onward(d, h) else 0

    def across(d, e, h):
        piece = a_all.at[others[d] * 2 + p, pl.ds(h * half, half)]
        return pltpu.make_async_remote_copy(
            src_ref=piece, dst_ref=piece,
            send_sem=load_sem.at[3], recv_sem=a_recv.at[halves(d + e, h)],
            device_id=(r, others[e], p), device_id_type=MESH)

    def sibling(d, h):
        piece = a_all.at[others[d] * 2 + p, pl.ds(h * half, half)]
        return pltpu.make_async_remote_copy(
            src_ref=piece, dst_ref=piece,
            send_sem=load_sem.at[3], recv_sem=sib_recv,
            device_id=(r, c, q), device_id_type=MESH)

    def await_blocks(count, sem):
        blocks = a_all.at[pl.ds(0, count)]
        pltpu.make_async_copy(blocks, blocks, sem).wait()

    def arrives(d, h):
        low, high = d & -d, 1 << (d.bit_length() - 1)
        e = low if h == 0 else high
        piece = a_all.at[others[d] * 2 + p, pl.ds(h * half, half)]
        pltpu.make_async_remote_copy(
            src_ref=piece, dst_ref=piece,
            send_sem=load_sem.at[3], recv_sem=a_recv.at[halves(d, h)],
            device_id=(r, others[e], p), device_id_type=MESH).wait_recv()
        for e in onward(d, h):
            across(d, e, h).start()
        sibling(d, h).start()

    def mask(block, j, domain):
        for t in range(spans[j].start // TILE, (spans[j].start + spans[j].size) // TILE):
            here = pl.ds(t * TILE, TILE)
            b_all[block, here, :] = b_all[block, here, :] * domain[t:t + 1, :].astype(jnp.bfloat16)

    @pl.when(r == 1)
    def _():
        for j in range(last):
            raw(j).start()

    for core in range(2):
        @pl.when(giver & (p == core))
        def _():
            cut(core).start()

    @pl.when((r == 1) & (c > 0))
    def _():
        raw(last).start()

    @pl.when(r > 0)
    def _():
        pl.semaphore_signal(above_in, inc=1, device_id=(r - 1, c, p), device_id_type=MESH)

    @pl.when(p == 1)
    def _():
        for e in bits:
            pl.semaphore_signal(plane_in, inc=1, device_id=(r, others[e], p), device_id_type=MESH)

    loads[0].wait()
    loads[1].wait()

    @pl.when(r == 1)
    def _():
        domains().start()

    for j in range(STRIPS):
        mask(r, j, dm_ref)

        @pl.when(r > 1)
        def _():
            down(r, 0, j).start()

    @pl.when(p == 1)
    def _():
        pl.semaphore_wait(plane_in, len(bits))
        pl.semaphore_signal(plane_in, inc=1, device_id=(r, c, q), device_id_type=MESH)

    def rise():
        @pl.when(r < R - 1)
        def _():
            pl.semaphore_wait(above_in, 1)
            for j in range(STRIPS):
                up(r, 0, j).start()

    @pl.when(p == 0)
    def _():
        rise()

    loads[2].wait()
    loads[3].wait()
    lane = lax.broadcasted_iota(jnp.int32, (1, width), 1) // TILE
    for t in range(rows // TILE):
        keep = jnp.zeros((1, width), jnp.float32)
        for u in range(width // TILE):
            keep = jnp.where(lane == u, im_ref[u:u + 1, t:t + 1].astype(jnp.float32), keep)
        here = pl.ds(t * TILE, TILE)
        a_all[me, here, :] = a_all[me, here, :] * keep.astype(jnp.bfloat16)

    @pl.when(p == 0)
    def _():
        pl.semaphore_wait(plane_in, 1)

    for core in range(2):
        @pl.when(giver & (p == core))
        def _():
            lend(core).start()

    for h in (1, 0):
        for e in bits:
            g = h if 2 * e < C else 1 - h
            across(0, e, g).start()
    for h in range(2):
        sibling(0, h).start()

    @pl.when(p == 1)
    def _():
        rise()

    pltpu.make_async_copy(energy, energy, load_sem.at[4]).wait()
    for t in range(rows // 128):
        v = jnp.broadcast_to(v_ref[:, t * 128:(t + 1) * 128], (128, 128)).T
        for u in range(cols // 128):
            lanes = slice(u * 128, (u + 1) * 128)
            factor = 1.0 / (v - o_ref[:, lanes])
            for w in range(128 // TILE):
                row = t * (128 // TILE) + w
                keep = dm_ref[row:row + 1, lanes].astype(jnp.float32)
                inv[pl.ds(row * TILE, TILE), lanes] = factor[w * TILE:(w + 1) * TILE] * keep

    def from_above(s, j):
        above = r + s + 1

        late = (s, j) == (0, last)

        @pl.when((above < R) & (r > 0) if late else above < R)
        def _():
            down(above, s, j).wait_recv()

            if s < R - 2:
                @pl.when(r > 0)
                def _():
                    down(above, s + 1, j).start()

        if s == 0 and not late:
            @pl.when(r == 0)
            def _():
                if j == 0:
                    domains().wait_recv()
                mask(1, j, dm_above)

    def from_below(s, j):
        below = r - s - 1

        @pl.when(below >= 0)
        def _():
            up(below, s, j).wait_recv()

            if s < R - 2:
                @pl.when(r < R - 1)
                def _():
                    up(below, s + 1, j).start()

    def product(block, j):
        return jnp.dot(a_all[block * parts + j], b_all[block, pl.ds(j * width, width), :],
                       preferred_element_type=jnp.float32)

    def add(s, j):
        @pl.when(r + s + 1 < R)
        def _():
            acc[...] += product(r + s + 1, j)

        @pl.when(r - s - 1 >= 0)
        def _():
            acc[...] += product(r - s - 1, j)

    each = [(s, j) for s in range(R - 2) for j in range(STRIPS)]
    strips = sorted([(i, from_above, *x) for i, x in enumerate(each)] + [(i + LAG, from_below, *x) for i, x in enumerate(each)],
                    key=lambda x: x[0])

    def take(count):
        for _ in range(min(count, len(strips))):
            _, take_from, s, j = strips.pop(0)
            take_from(s, j)

    order = sorted(relayed, key=lambda x: (x[0].bit_count(), x[1] if 2 * x[0] >= C else 1 - x[1]))
    take(6)
    for d, h in order:
        arrives(d, h)

    for core in range(2):
        @pl.when(helper[core])
        def _():
            lend(core).wait_recv()
            pass_on(core).start()

    take(6)
    await_blocks(len(leaves) // 2, a_recv.at[0])
    for d, h in leaves:
        sibling(d, h).start()
    take(len(strips))

    @pl.when(r == 0)
    def _():
        down(1, 0, last).wait_recv()
        mask(1, last, dm_above)

    await_blocks(C, sib_recv)

    acc[...] = product(r, 0)
    for j in range(1, parts):
        acc[...] += product(r, j)
    for s in range(R - 2):
        for j in range(parts):
            add(s, j)

    def most(block):
        for j in range(parts - 1):
            acc[...] += product(block, j)
        k = (parts - 1) * width
        if tall < width:
            acc[...] += jnp.dot(a_all[block * parts + parts - 1, :, :width - tall], b_all[block, k:depth - tall, :],
                                preferred_element_type=jnp.float32)

    def strips_of(block):
        return b_all.at[block, pl.ds(0, depth - tall)]

    @pl.when(r == 0)
    def _():
        pltpu.make_async_copy(strips_of(R - 1), strips_of(R - 1), b_recv.at[place[0, R - 2, 0]]).wait()
        most(R - 1)

    @pl.when(r == R - 1)
    def _():
        pltpu.make_async_copy(strips_of(0), strips_of(0), b_recv.at[place[1, R - 2, 0]]).wait()
        most(0)

    await_blocks(2 * C - 1, load_sem.at[3])

    @pl.when((r == 0) | (r == R - 1))
    def _():
        await_blocks(1, b_sent)

    from_above(R - 2, last)
    from_below(R - 2, last)

    def finish(block):
        k = depth - tall
        term = jnp.dot(a_all[block * parts + parts - 1, :, width - tall:], b_all[block, k:k + tall, :],
                       preferred_element_type=jnp.float32)
        acc[...] = (acc[...] + term) * inv[...]

    @pl.when(r == 0)
    def _():
        finish(R - 1)

    @pl.when(r == R - 1)
    def _():
        finish(0)

    @pl.when((r > 0) & (r < R - 1))
    def _():
        acc[...] = acc[...] * inv[...]
        await_blocks(R + 1, b_sent)

    @pl.when(r == 1)
    def _():
        domains().wait_send()

    for core in range(2):
        @pl.when(helper[core])
        def _():
            pass_on(core).wait_send()


def solution(mesh):
    R, C = mesh.shape["row"], mesh.shape["col"]

    def local(integrals, int_mask, amplitudes, domain_mask, virt_energy, occ_energy):
        rows, width = integrals.shape
        depth, cols = amplitudes.shape
        hbm = pl.BlockSpec(memory_space=pl.ANY)
        dma = pltpu.SemaphoreType.DMA
        relays = sum(bool(passes(C, d, h)) for d in range(1, C) for h in range(2))
        operands = (integrals, int_mask.T, amplitudes, domain_mask,
                    virt_energy.reshape(1, rows), occ_energy.reshape(1, cols))
        return pl.pallas_call(
            functools.partial(kernel, R, C),
            out_shape=pltpu.VMEM((rows, cols), jnp.float32),
            in_specs=[hbm] * 6,
            out_specs=pl.BlockSpec(memory_space=pltpu.VMEM),
            scratch_shapes=[
                pltpu.VMEM((C * 2, rows, width), jnp.bfloat16),
                pltpu.VMEM((R, depth, cols), jnp.bfloat16),
                pltpu.VMEM((rows, cols), jnp.float32),
                pltpu.VMEM(int_mask.shape[::-1], jnp.int32),
                pltpu.VMEM(domain_mask.shape, jnp.int32),
                pltpu.VMEM(domain_mask.shape, jnp.int32),
                pltpu.VMEM((1, rows + cols), jnp.float32),
                pltpu.VMEM((sum(LENT), cols), jnp.bfloat16),
                dma((5,)), dma((1 + relays,)), dma, dma, dma, dma((arrivals(R)[1],)), dma,
                pltpu.SemaphoreType.REGULAR, pltpu.SemaphoreType.REGULAR,
            ],
            compiler_params=pltpu.CompilerParams(
                collective_id=0, has_side_effects=True, vmem_limit_bytes=32 * 2**20),
            cost_estimate=pl.CostEstimate(
                flops=2 * rows * depth * R * cols, bytes_accessed=4 * 2**20, transcendentals=0),
        )(*[pltpu.with_memory_space_constraint(x, pltpu.HBM) for x in operands])

    placed = (
        P("row", ("col", "pair")),
        P("row", ("col", "pair")),
        P("row", ("col", "pair")),
        P("row", ("col", "pair")),
        P("row"),
        P(("col", "pair")),
    )
    return jax.shard_map(
        local, mesh=mesh, in_specs=placed, out_specs=P("row", ("col", "pair")), check_vma=False
    )
```
